32 devices in a mesh: dp: 8 (over z, x), mp: 4 (over y, core).
Axes of the slice: x: 2, y: 2, z: 4, core: 2. Of those that a mesh axis runs over, the one named last changes fastest.
Arguments:
- inputs: bfloat16 [16, 512, 768], P('dp', 'mp'), may hold values from -6 to 6
- w_qkv: bfloat16 [3, 768, 768], P(None, 'dp', 'mp'), may hold values from -0.21875 to 0.21875
- w_out: bfloat16 [768, 768], P('mp', 'dp'), may hold values from -1.75 to 1.75
- w_up: bfloat16 [768, 3072], P('dp', 'mp'), may hold values from -0.21875 to 0.21875
- w_down: bfloat16 [3072, 768], P('mp', 'dp'), may hold values from -0.109375 to 0.109375
- unit_bias: bfloat16 [4, 1152], P('mp', 'dp'), may hold values from -3 to 3
- norm_gain: bfloat16 [2, 768], P(None, ('dp', 'mp')), may hold values from 0.25 to 1.75
- norm_bias: bfloat16 [4, 768], P(None, ('dp', 'mp')), may hold values from -3 to 3
- seq_lengths: int32 [16, 4], P('dp'), may hold values from 0 to 512, as said below
- cotangent: bfloat16 [16, 512, 768], P('dp', 'mp'), may hold values from -6 to 6
Outputs:
- outputs: bfloat16 [16, 512, 768], P('dp', 'mp')
- grad_inputs: float32 [16, 512, 768], P('dp', 'mp')
- grad_qkv: float32 [3, 768, 768], P(None, 'dp', 'mp')
- grad_out: float32 [768, 768], P('mp', 'dp')
- grad_up: float32 [768, 3072], P('dp', 'mp')
- grad_down: float32 [3072, 768], P('mp', 'dp')
- grad_unit_bias: float32 [4, 1152], P('mp', 'dp')
- grad_gain: float32 [2, 768], P(None, ('dp', 'mp'))
- grad_bias: float32 [4, 768], P(None, ('dp', 'mp'))
The draws below stay inside these ranges and needn't reach their ends.
Inputs may be any that keep to these rules, and one draw needn't show every extreme that they name: `seq_lengths`: each row lists the lengths of 4 sequences packed from the first row of a micro-batch of 512 rows, zero for an unused slot; a row's lengths sum to at most 512, and the rows after that sum are padding.
All inputs are finite; a program needn't handle non-finite values.
Results may differ from the reference program's by a relative error of at most 0.02.
Values may be sent and summed in bfloat16 or wider, within the bound.
No kernel may reach another device: no remote copies, remote signals or barrier semaphores. Data moves between devices by JAX's collectives and lax.ppermute only.
A program may use at most 128 MiB of HBM per device.

```python
import jax
import jax.numpy as jnp
from jax import lax

D = 768
HEADS = 12
HD = 64
FF = 3072
ROWS = 512
SLOTS = 4
MICRO = 16
BIAS_ROWS = 4
BIAS_MP = 1152
N_MP = 4


def draw_seq_lengths(key, part):
    key = jax.random.fold_in(key, 11)
    first_key, second_key, third_key = jax.random.split(key, 3)
    small_cap = ROWS // (4 * SLOTS)
    others = jax.random.randint(first_key, (MICRO, SLOTS), 1, small_cap + 1, dtype=jnp.int32)
    long_slot = jax.random.randint(second_key, (MICRO, 1), 0, SLOTS, dtype=jnp.int32)
    is_long = jnp.arange(SLOTS, dtype=jnp.int32)[None, :] == long_slot
    others = jnp.where(is_long, 0, others)
    remainder = jnp.sum(others, axis=1, keepdims=True, dtype=jnp.int32)
    lowest = 3 * ROWS // 4 + 1
    room_left = ROWS - remainder - lowest + 1
    addition = jax.random.randint(third_key, (MICRO, 1), 0, 1 << 20, dtype=jnp.int32) % room_left
    lengths = jnp.where(is_long, lowest + addition, others).astype(jnp.int32)
    first_line = jnp.where(is_long[0], ROWS, 0).astype(jnp.int32)
    return lengths.at[0].set(first_line)


def level_of(own_key, dims, cuts, low, top_value):
    def one(dim, blocks):
        steps = jax.random.uniform(jax.random.fold_in(jax.random.fold_in(own_key, 6), dim), (blocks,), jnp.float32, low / len(cuts), top_value / len(cuts))
        return jnp.repeat(jnp.exp(steps), dims[dim] // blocks).reshape((-1,) + (1,) * (len(dims) - dim - 1))

    factor_of = one(*cuts[0])
    for cut in cuts[1:]:
        factor_of = factor_of * one(*cut)
    return factor_of


def bell_draw(own_key, dims, scale, reach, pieces=(), held_as=jnp.bfloat16):
    gain = level_of(own_key, dims, pieces, -0.22, 0.18) if pieces else 1.0
    values = jax.random.normal(own_key, dims, jnp.float32) * scale * gain
    return jnp.minimum(jnp.maximum(values, -reach), reach).astype(held_as)


def setup_inputs(seed: int = 0) -> dict:
    streams_of = jax.random.split(jax.random.key(seed), 11)
    inputs = bell_draw(streams_of[0], (MICRO, ROWS, D), 1.0, 6.0, ((0, 8), (1, 4)))
    w_qkv = bell_draw(streams_of[1], (3, D, D), D ** -0.5, 0.21875, ((1, 8), (2, 4)))
    w_out = bell_draw(streams_of[2], (D, D), (D // 64 + 1) ** -0.5, 1.75, ((0, 4), (1, 8)))
    w_up = bell_draw(streams_of[3], (D, FF), D ** -0.5, 0.21875, ((0, 8), (1, 4)))
    w_down = bell_draw(streams_of[4], (FF, D), FF ** -0.5, 0.109375, ((0, 4), (1, 8)))
    unit_bias = bell_draw(streams_of[5], (BIAS_ROWS, BIAS_MP), 0.5, 3.0, ((0, 4), (1, 8)))
    norm_gain = jnp.clip(1.0 + 0.15 * jax.random.normal(streams_of[6], (2, D), jnp.float32), 0.25, 1.75).astype(jnp.bfloat16)
    norm_bias = bell_draw(streams_of[7], (4, D), 0.5, 3.0, ((1, 32),))
    seq_lengths = draw_seq_lengths(jax.random.fold_in(streams_of[10], 71), 0)
    cotangent = bell_draw(streams_of[9], (MICRO, ROWS, D), 1.0, 6.0, ((0, 8), (1, 4)))
    return dict(inputs=inputs, w_qkv=w_qkv, w_out=w_out, w_up=w_up, w_down=w_down, unit_bias=unit_bias, norm_gain=norm_gain, norm_bias=norm_bias, seq_lengths=seq_lengths, cotangent=cotangent)


@jax.custom_vjp
def low(v):
    return lax.optimization_barrier(v.astype(jnp.bfloat16)).astype(jnp.float32)

@jax.custom_vjp
def low_back(v):
    return v

def low_keep(v):
    return (low(v), None)

def low_pass(kept, grad):
    return (grad,)

def back_keep(v):
    return (v, None)

def back_low(kept, grad):
    return (low(grad),)
low.defvjp(low_keep, low_pass)
low_back.defvjp(back_keep, back_low)
exact_mode = lax.Precision.HIGHEST

def segment_ids(lengths, total_rows):
    bounds = jnp.cumsum(lengths, dtype=jnp.int32)
    places = jnp.arange(total_rows, dtype=jnp.int32)
    return lax.optimization_barrier(jnp.sum((places[:, None] >= bounds[None, :]).astype(jnp.int32), axis=1, dtype=jnp.int32))

def layer_norm(values, scales, offsets):
    average = lax.optimization_barrier(jnp.mean(values, axis=-1, keepdims=True))
    centred = values - average
    spread = lax.optimization_barrier(jnp.mean(centred * centred, axis=-1, keepdims=True))
    return centred * lax.rsqrt(spread + 1e-06) * scales + offsets

def forward(inputs, w_qkv, w_out, w_up, w_down, unit_bias, norm_gain, norm_bias, seq_lengths):
    head_cols = D // N_MP
    q_bias = unit_bias[:, :head_cols].reshape(D)
    v_bias = unit_bias[:, head_cols:2 * head_cols].reshape(D)
    up_bias = unit_bias[:, 2 * head_cols:].reshape(FF)
    score_scale = HD ** (-0.5)

    def encoder_block(scan_state, scan_item):
        rows_in, lengths = scan_item
        labels = segment_ids(lengths, ROWS)
        allowed = labels[:, None] == labels[None, :]
        projected = jnp.einsum('rd,tde->tre', rows_in, w_qkv, precision=exact_mode)
        queries = low(low_back(projected[0] + q_bias)).reshape(ROWS, HEADS, HD)
        keys_all = low(low_back(projected[1])).reshape(ROWS, HEADS, HD)
        values_all = low(low_back(projected[2] + v_bias)).reshape(ROWS, HEADS, HD)
        scores = low_back(jnp.einsum('qhe,khe->hqk', queries, keys_all, precision=exact_mode) * score_scale)
        scores = jnp.where(allowed[None], scores, -1000000000.0)
        weights = low(jax.nn.softmax(scores, axis=-1))
        context = jnp.einsum('hqk,khe->qhe', weights, values_all, precision=exact_mode).reshape(ROWS, D)
        context = low(low_back(context))
        attended = low_back(jnp.dot(context, w_out, precision=exact_mode))
        normed_first = layer_norm(rows_in + attended + norm_bias[0], norm_gain[0], norm_bias[1])
        hidden = low_back(jnp.dot(low(normed_first), w_up, precision=exact_mode) + up_bias)
        activated = low(jax.nn.gelu(hidden, approximate=False))
        mlp_out = low_back(jnp.dot(activated, w_down, precision=exact_mode))
        result = layer_norm(normed_first + mlp_out + norm_bias[2], norm_gain[1], norm_bias[3])
        return (scan_state, result)
    scan_state, result = lax.scan(jax.checkpoint(encoder_block), jnp.float32(0.0), (inputs, seq_lengths))
    return result

def reference(inputs, w_qkv, w_out, w_up, w_down, unit_bias, norm_gain, norm_bias, seq_lengths, cotangent):
    floats = (inputs.astype(jnp.float32), w_qkv.astype(jnp.float32), w_out.astype(jnp.float32), w_up.astype(jnp.float32), w_down.astype(jnp.float32), unit_bias.astype(jnp.float32), norm_gain.astype(jnp.float32), norm_bias.astype(jnp.float32))

    def closed(inputs_f, qkv_f, out_f, up_f, down_f, unit_f, gain_f, bias_f):
        return forward(inputs_f, qkv_f, out_f, up_f, down_f, unit_f, gain_f, bias_f, seq_lengths)
    result, pullback = jax.vjp(closed, *floats)
    gradients = pullback(cotangent.astype(jnp.float32))
    return (result.astype(jnp.bfloat16), gradients[0], gradients[1], gradients[2], gradients[3], gradients[4], gradients[5], gradients[6], gradients[7])
```

```python
import jax
import jax.numpy as jnp
from jax import lax
from jax.sharding import PartitionSpec as P

HD = 64
EXTRA = 16
BF = jnp.bfloat16
F32 = jnp.float32


def dot(left, right, dims):
    return lax.dot_general(left, right, (dims, ((), ())), preferred_element_type=F32)


class Place:
    def __init__(self):
        self.groups = lax.axis_size("dp")
        self.line_size = self.groups // 2
        data, model = lax.axis_index("dp"), lax.axis_index("mp")
        self.line, self.pair = data // 2, data % 2
        self.row, self.core = model // 2, model % 2

    def core_swap(self, value):
        return lax.ppermute(value, "mp", [(0, 1), (1, 0), (2, 3), (3, 2)])

    def row_swap(self, value):
        return lax.ppermute(value, "mp", [(0, 2), (2, 0), (1, 3), (3, 1)])

    def line_shift(self, value, step):
        n = self.line_size
        pairs = [(i * 2 + j, ((i + step) % n) * 2 + j) for i in range(n) for j in range(2)]
        return lax.ppermute(value, "dp", pairs)

    def cross(self, value, along_row):
        pairs = []
        for data in range(self.groups):
            for model in range(4):
                if model % 2 == along_row:
                    pairs.append((data * 4 + model, data * 4 + (model ^ 2)))
                else:
                    pairs.append((data * 4 + model, (data ^ 1) * 4 + model))
        return lax.ppermute(value, ("dp", "mp"), pairs)

    def quarters(self):
        other_row, other_pair = 1 - self.row, 1 - self.pair
        swap = self.core == 0
        first = (jnp.where(swap, other_row, self.row), jnp.where(swap, self.pair, other_pair))
        second = (jnp.where(swap, self.row, other_row), jnp.where(swap, other_pair, self.pair))
        return (self.row, self.pair), first, second, (other_row, other_pair)


def gather_group(place, shard):
    n = place.line_size
    parts = [shard] + [place.line_shift(shard, step) for step in range(1, n)]
    own = jnp.stack(parts)
    first = place.cross(own, 0)
    rest = place.cross(jnp.stack([own, first]), 1)
    whole = jnp.zeros((2, n, 2) + shard.shape, shard.dtype)
    for piece, (row, pair) in zip((own, first, rest[0], rest[1]), place.quarters()):
        for step in range(n):
            start = (row, (place.line - step) % n, pair, 0, 0)
            whole = lax.dynamic_update_slice(whole, piece[step][None, None, None], start)
    return whole


def scatter_group(place, terms):
    n = place.line_size

    def quarter(at):
        row, pair = at
        size = (1, n, 1) + terms.shape[3:]
        return lax.dynamic_slice(terms, (row, 0, pair, 0, 0), size).reshape((n,) + terms.shape[3:])

    own, first, second, far = (quarter(at) for at in place.quarters())
    got = place.cross(jnp.stack([first, far]).astype(BF), 0)
    second = second.astype(F32) + got[1].astype(F32)
    got_second = place.cross(second.astype(BF), 1)
    own = own.astype(F32) + got[0].astype(F32) + got_second.astype(F32)
    own_low = own.astype(BF)
    total = lax.dynamic_index_in_dim(own, place.line, 0, keepdims=False)
    for step in range(1, n):
        send = lax.dynamic_index_in_dim(own_low, (place.line + step) % n, 0, keepdims=False)
        total = total + place.line_shift(send, step).astype(F32)
    return total


def norm_parts(values):
    centred = values - jnp.mean(values, axis=-1, keepdims=True)
    rate = lax.rsqrt(jnp.mean(centred * centred, axis=-1, keepdims=True) + 1e-06)
    return centred * rate, rate


def norm_back(grad, unit, rate, scale):
    inner = grad * scale
    return rate * (
        inner
        - jnp.mean(inner, axis=-1, keepdims=True)
        - unit * jnp.mean(inner * unit, axis=-1, keepdims=True)
    )


def body(
    inputs, w_qkv, w_out, w_up, w_down, unit_bias, norm_gain, norm_bias, seq_lengths, cotangent
):
    place = Place()
    n, row, core = place.line_size, place.row, place.core
    groups = place.groups
    block, width = inputs.shape[1], inputs.shape[2]
    rows = 4 * block
    depth, head_cols = w_qkv.shape[1], w_qkv.shape[2]
    units = w_up.shape[1]
    share = unit_bias.shape[1]
    small = norm_gain.shape[1]
    heads = 2 * head_cols // HD
    scale = HD ** (-0.5)

    keep = lambda array, index: lax.dynamic_index_in_dim(array, index, 0, keepdims=False)
    outgoing = jnp.stack([keep(inputs, 1 - row), keep(cotangent, 1 - row)])
    incoming = place.row_swap(outgoing)
    mine = jnp.stack([keep(inputs, row), keep(cotangent, row)])
    low_rows = jnp.where(row == 0, mine, incoming)
    high_rows = jnp.where(row == 0, incoming, mine)
    half = jnp.concatenate([low_rows, high_rows], axis=1)
    other = place.core_swap(half)
    both = jnp.where(
        core == 0,
        jnp.concatenate([half, other], axis=1),
        jnp.concatenate([other, half], axis=1),
    )
    x, grad_rows = both[0], both[1]

    vector = jnp.concatenate([unit_bias[0], norm_gain.reshape(-1), norm_bias.reshape(-1)])
    vector = jnp.pad(vector[None], ((0, EXTRA - 1), (0, width - vector.shape[0])))
    first_shard = jnp.concatenate(
        [w_qkv[0], w_qkv[1], w_qkv[2], jnp.transpose(w_out)], axis=1
    )
    first_whole = gather_group(place, jnp.concatenate([first_shard, vector], axis=0))
    up_whole = gather_group(place, w_up).reshape(2, width, units)
    down_whole = gather_group(place, jnp.transpose(w_down)).reshape(2, width, units)
    attn_whole = first_whole[:, :, :, :depth].reshape(2, width, width)
    vectors = first_whole[:, :, :, depth, : share + 6 * small].reshape(2, groups, -1)
    unit_values = vectors[:, :, :share].reshape(2, groups * share).astype(F32)
    norm_here = vectors[:, :, share:]
    norm_there = place.core_swap(norm_here)
    norm_all = jnp.where(
        core == 0,
        jnp.stack([norm_here, norm_there], axis=2),
        jnp.stack([norm_there, norm_here], axis=2),
    )
    norm_all = norm_all.reshape(2, groups, 2, 6, small)
    norm_all = jnp.transpose(norm_all, (3, 1, 0, 2, 4)).reshape(6, width).astype(F32)
    gains, offsets = norm_all[:2], norm_all[2:]
    q_bias = unit_values[:, :head_cols].reshape(-1)
    v_bias = unit_values[:, head_cols : 2 * head_cols].reshape(-1)
    up_bias = unit_values[:, 2 * head_cols :].reshape(-1)

    lengths = keep(seq_lengths, row)
    bounds = jnp.cumsum(lengths, dtype=jnp.int32)
    ids = jnp.arange(rows, dtype=jnp.int32).reshape(2, 2, block)
    places = jnp.transpose(ids, (1, 0, 2)).reshape(rows)
    labels = jnp.sum((places[:, None] >= bounds[None, :]).astype(jnp.int32), axis=1)
    allowed = labels[:, None] == labels[None, :]

    def columns(index):
        lo = index * head_cols
        return attn_whole[:, :, lo : lo + head_cols]

    def project(index):
        parts = [dot(x, columns(index)[j], ((1,), (0,))) for j in range(2)]
        return jnp.concatenate(parts, axis=1)

    def split(flat):
        return flat.reshape(rows, heads, HD)

    queries = split((project(0) + q_bias).astype(BF))
    keys = split(project(1).astype(BF))
    values = split((project(2) + v_bias).astype(BF))
    scores = jnp.einsum("qhe,khe->hqk", queries, keys, preferred_element_type=F32) * scale
    scores = jnp.where(allowed[None], scores, -1000000000.0)
    peak = jnp.max(scores, axis=-1, keepdims=True)
    exponent = jnp.exp(scores - peak)
    probs = exponent / jnp.sum(exponent, axis=-1, keepdims=True)
    probs_low = probs.astype(BF)
    context = jnp.einsum("hqk,khe->qhe", probs_low, values, preferred_element_type=F32)
    context = context.reshape(rows, 2 * head_cols).astype(BF)
    w_out_t = [columns(3)[j] for j in range(2)]
    attended = dot(context[:, :head_cols], w_out_t[0], ((1,), (1,))) + dot(
        context[:, head_cols:], w_out_t[1], ((1,), (1,))
    )

    def pair_sum(partial):
        low = partial.astype(BF)
        return low.astype(F32) + place.core_swap(low).astype(F32)

    first_in = x.astype(F32) + pair_sum(attended) + offsets[0]
    unit_one, rate_one = norm_parts(first_in)
    normed_first = unit_one * gains[0] + offsets[1]
    first_low = normed_first.astype(BF)
    hidden = jnp.concatenate(
        [dot(first_low, up_whole[j], ((1,), (0,))) for j in range(2)], axis=1
    ) + up_bias
    cdf = 0.5 * lax.erfc(-hidden * (0.5**0.5))
    activated = (hidden * cdf).astype(BF)
    slope = cdf + hidden * jnp.exp(-0.5 * hidden * hidden) * 0.3989422804014327
    down = sum(
        dot(activated[:, j * units : (j + 1) * units], down_whole[j], ((1,), (1,)))
        for j in range(2)
    )
    second_in = normed_first + pair_sum(down) + offsets[2]
    unit_two, rate_two = norm_parts(second_in)
    result = (unit_two * gains[1] + offsets[3]).astype(BF)

    dy = grad_rows.astype(F32)
    d_second = norm_back(dy, unit_two, rate_two, gains[1])
    d_mixed = d_second.astype(BF)

    def outer(left, right):
        return dot(left, right, ((0,), (0,))).astype(BF)

    def shaped(terms):
        return jnp.stack(terms).reshape(2, n, 2, depth, -1)

    down_terms = shaped(
        [outer(d_mixed, activated[:, j * units : (j + 1) * units]) for j in range(2)]
    )
    grad_down = jnp.transpose(scatter_group(place, down_terms))
    d_activated = jnp.concatenate(
        [dot(d_mixed, down_whole[j], ((1,), (0,))) for j in range(2)], axis=1
    )
    d_hidden = (d_activated * slope).astype(BF)
    up_terms = shaped(
        [outer(first_low, d_hidden[:, j * units : (j + 1) * units]) for j in range(2)]
    )
    grad_up = scatter_group(place, up_terms)
    d_up_bias = jnp.sum(d_hidden.astype(F32), axis=0)
    d_normed = sum(
        dot(d_hidden[:, j * units : (j + 1) * units], up_whole[j], ((1,), (1,)))
        for j in range(2)
    )
    d_first = d_second + pair_sum(d_normed)
    d_first_in = norm_back(d_first, unit_one, rate_one, gains[0])
    d_attended = d_first_in.astype(BF)
    d_context = jnp.concatenate(
        [dot(d_attended, w_out_t[j], ((1,), (0,))) for j in range(2)], axis=1
    )
    d_context = split(d_context.astype(BF))
    d_probs = jnp.einsum("qhe,khe->hqk", d_context, values, preferred_element_type=F32)
    d_values = jnp.einsum("hqk,qhe->khe", probs_low, d_context, preferred_element_type=F32)
    inner = jnp.sum(d_probs * probs, axis=-1, keepdims=True)
    d_scores = (probs * (d_probs - inner)).astype(BF)
    d_queries = jnp.einsum("hqk,khe->qhe", d_scores, keys, preferred_element_type=F32) * scale
    d_keys = jnp.einsum("hqk,qhe->khe", d_scores, queries, preferred_element_type=F32) * scale
    flat = lambda array: array.reshape(rows, 2 * head_cols).astype(BF)
    d_queries, d_keys, d_values = flat(d_queries), flat(d_keys), flat(d_values)
    d_parts = []
    for j in range(2):
        cut = slice(j * head_cols, (j + 1) * head_cols)
        d_parts.append(jnp.concatenate([d_queries[:, cut], d_keys[:, cut], d_values[:, cut]], axis=1))
    attn_terms = shaped(
        [
            jnp.concatenate(
                [
                    outer(x, d_parts[j]),
                    outer(d_attended, context[:, j * head_cols : (j + 1) * head_cols]),
                ],
                axis=1,
            )
            for j in range(2)
        ]
    )
    total = lambda array: jnp.sum(array.astype(F32), axis=0)
    unit_terms = jnp.concatenate(
        [
            total(d_queries).reshape(2, head_cols),
            total(d_values).reshape(2, head_cols),
            d_up_bias.reshape(2, units),
        ],
        axis=1,
    ).reshape(2, groups, share)
    norm_terms = jnp.stack(
        [
            total(d_first * unit_one),
            total(dy * unit_two),
            total(d_first_in),
            total(d_first),
            total(d_second),
            total(dy),
        ]
    ).reshape(6, groups, 2, 2, small)
    norm_terms = lax.dynamic_index_in_dim(norm_terms, core, 3, keepdims=False)
    norm_terms = jnp.transpose(norm_terms, (2, 1, 0, 3)).reshape(2, groups, 6 * small)
    vector_terms = jnp.concatenate([unit_terms, norm_terms], axis=2)
    vector_terms = jnp.pad(
        vector_terms[:, :, None],
        ((0, 0), (0, 0), (0, EXTRA - 1), (0, width - vector_terms.shape[2])),
    ).reshape(2, n, 2, EXTRA, width)
    attn_grad = scatter_group(
        place, jnp.concatenate([attn_terms, vector_terms.astype(BF)], axis=3)
    )
    d_inputs = sum(
        dot(d_parts[j], attn_whole[j][:, : 3 * head_cols], ((1,), (1,))) for j in range(2)
    )
    grad_in = d_first_in + pair_sum(d_inputs)

    def hand_back(full):
        mine = lax.dynamic_slice_in_dim(full, core * 2 * block, 2 * block, 0)
        mine = mine.reshape(2, block, width)
        kept = keep(mine, row)
        got = place.row_swap(keep(mine, 1 - row).astype(BF)).astype(full.dtype)
        return jnp.where(row == 0, jnp.stack([kept, got]), jnp.stack([got, kept]))

    grad_qkv = jnp.stack(
        [attn_grad[:depth, t * head_cols : (t + 1) * head_cols] for t in range(3)]
    )
    grad_out = jnp.transpose(attn_grad[:depth, 3 * head_cols :])
    vector_grad = attn_grad[depth]
    norm_grad = vector_grad[share : share + 6 * small].reshape(6, small)
    return (
        hand_back(result),
        hand_back(grad_in),
        grad_qkv,
        grad_out,
        grad_up,
        grad_down,
        vector_grad[None, :share],
        norm_grad[:2],
        norm_grad[2:],
    )


def solution(mesh):
    placed = (
        P("dp", "mp", None),
        P(None, "dp", "mp"),
        P("mp", "dp"),
        P("dp", "mp"),
        P("mp", "dp"),
        P("mp", "dp"),
        P(None, ("dp", "mp")),
        P(None, ("dp", "mp")),
        P("dp", None),
        P("dp", "mp", None),
    )
    return jax.shard_map(
        body,
        mesh=mesh,
        in_specs=placed,
        out_specs=(
            P("dp", "mp", None),
            P("dp", "mp", None),
            P(None, "dp", "mp"),
            P("mp", "dp"),
            P("dp", "mp"),
            P("mp", "dp"),
            P("mp", "dp"),
            P(None, ("dp", "mp")),
            P(None, ("dp", "mp")),
        ),
        check_vma=False,
    )
```

```python
import functools

import jax
import jax.numpy as jnp
from jax import lax
from jax.experimental import pallas as pl
from jax.experimental.pallas import tpu as pltpu
from jax.sharding import PartitionSpec as P

HD = 64
LANES = 128
EXTRA = 16
BF = jnp.bfloat16
F32 = jnp.float32
LIMIT = 56 * 1024 * 1024
NN = ((1,), (0,))
NT = ((1,), (1,))
TN = ((0,), (0,))


def dot(left, right, dims=NN):
    return lax.dot_general(left, right, (dims, ((), ())), preferred_element_type=F32)


def call(kernel, outs, args, scalars=0, scratch=(), flops=0):
    return pl.pallas_call(
        kernel,
        out_shape=[jax.ShapeDtypeStruct(shape, kind) for shape, kind in outs],
        in_specs=[pl.BlockSpec(memory_space=pltpu.SMEM)] * scalars
        + [pl.BlockSpec(memory_space=pltpu.VMEM)] * (len(args) - scalars),
        out_specs=[pl.BlockSpec(memory_space=pltpu.VMEM)] * len(outs),
        scratch_shapes=list(scratch),
        compiler_params=pltpu.CompilerParams(vmem_limit_bytes=LIMIT),
        cost_estimate=pl.CostEstimate(
            flops=flops,
            bytes_accessed=sum(a.size * a.dtype.itemsize for a in args),
            transcendentals=0,
        ),
    )(*args)


class Place:
    def __init__(self):
        self.groups = lax.axis_size("dp")
        self.line_size = self.groups // 2
        data, model = lax.axis_index("dp"), lax.axis_index("mp")
        self.line, self.pair = data // 2, data % 2
        self.row, self.core = model // 2, model % 2

    def core_swap(self, value):
        return lax.ppermute(value, "mp", [(0, 1), (1, 0), (2, 3), (3, 2)])

    def row_swap(self, value):
        return lax.ppermute(value, "mp", [(0, 2), (2, 0), (1, 3), (3, 1)])

    def line_swap(self, value, step):
        pairs = [(i, i ^ (2 * step)) for i in range(self.groups)]
        return lax.ppermute(value, "dp", pairs)

    def cross(self, value, along_row):
        pairs = []
        for data in range(self.groups):
            for model in range(4):
                if model % 2 == along_row:
                    pairs.append((data * 4 + model, data * 4 + (model ^ 2)))
                else:
                    pairs.append((data * 4 + model, (data ^ 1) * 4 + model))
        return lax.ppermute(value, ("dp", "mp"), pairs)

    def quarters(self):
        other_row, other_pair = 1 - self.row, 1 - self.pair
        swap = self.core == 0
        first = (jnp.where(swap, other_row, self.row), jnp.where(swap, self.pair, other_pair))
        second = (jnp.where(swap, self.row, other_row), jnp.where(swap, other_pair, self.pair))
        return (self.row, self.pair), first, second, (other_row, other_pair)

    def scatter_table(self):
        flags, slots = [], []
        for row in range(2):
            for pair in range(2):
                same_row, same_pair = self.row == row, self.pair == pair
                own = same_row & same_pair
                far = ~same_row & ~same_pair
                first = jnp.where(self.core == 0, ~same_row & same_pair, same_row & ~same_pair)
                flags.append((far | first).astype(jnp.int32))
                slots.append((far | ~(own | first | far)).astype(jnp.int32))
        return jnp.stack(flags + slots + [self.line]).astype(jnp.int32)


def gather_line(place, shard):
    n = place.line_size
    if n <= 4:
        return jnp.stack([shard] + [place.line_swap(shard, step) for step in range(1, n)])
    held, step = shard[None], 1
    while step < n:
        held, step = jnp.concatenate([held, place.line_swap(held, step)]), step * 2
    return held


def scatter_line(place, terms):
    n = place.line_size
    if n <= 4:
        low = terms.astype(BF)
        total = terms[0]
        for step in range(1, n):
            total = total + place.line_swap(low[step], step).astype(F32)
        return total
    step = n // 2
    while step:
        got = place.line_swap(terms[step:].astype(BF), step)
        terms, step = terms[:step] + got.astype(F32), step // 2
    return terms[0]


def place_kernel(depth, n, extra, where, own, first, rest, whole, *more):
    for quarter in range(4):
        row, pair = where[2 * quarter], where[2 * quarter + 1]
        source = (own, first, rest.at[0], rest.at[1])[quarter]
        for step in range(n):
            data = jnp.bitwise_xor(where[8], step) * 2 + pair
            start = pl.multiple_of(data * depth, 16)
            whole[row, pl.ds(start, depth), :] = source[step, :depth]
            if extra:
                more[0][row, data] = source[step, depth:]


def gather_group(place, own, depth):
    n, rows, width = own.shape
    first = place.cross(own, 0)
    rest = place.cross(jnp.stack([own, first]), 1)
    extra = rows > depth
    if depth % 16 == 0:
        spots = [scalar for spot in place.quarters() for scalar in spot] + [place.line]
        outs = [((2, 2 * n * depth, width), own.dtype)]
        if extra:
            outs.append(((2, 2 * n, EXTRA, width), own.dtype))
        return call(
            functools.partial(place_kernel, depth, n, extra),
            outs,
            [jnp.stack(spots).astype(jnp.int32), own, first, rest],
            scalars=1,
        )
    whole = jnp.zeros((2, n, 2, rows, width), own.dtype)
    for piece, (row, pair) in zip((own, first, rest[0], rest[1]), place.quarters()):
        for step in range(n):
            start = (row, place.line ^ step, pair, 0, 0)
            whole = lax.dynamic_update_slice(whole, piece[step][None, None, None], start)
    out = [whole[:, :, :, :depth].reshape(2, 2 * n * depth, width)]
    if extra:
        out.append(whole[:, :, :, depth:].reshape(2, 2 * n, EXTRA, width))
    return out


def spread(place, terms, depth, vectors=None):
    n = place.line_size
    terms = terms.reshape(2, n, 2, depth, terms.shape[-1])
    if vectors is not None:
        vectors = jnp.broadcast_to(vectors.reshape(2, n, 2, 1, -1), (2, n, 2, EXTRA, vectors.shape[-1]))
        terms = jnp.concatenate([terms, vectors.astype(terms.dtype)], axis=3)
    order = lax.iota(jnp.int32, n) ^ place.line
    terms = jnp.take(terms, order, axis=1)

    def quarter(at):
        size = (1, n, 1) + terms.shape[3:]
        return lax.dynamic_slice(terms, (at[0], 0, at[1], 0, 0), size).reshape((n,) + terms.shape[3:])

    own, first, second, far = (quarter(at) for at in place.quarters())
    return jnp.stack([first, far]), jnp.stack([own, second])


def scatter_group(place, send, keep):
    got = place.cross(send, 0)
    second = (keep[1].astype(F32) + got[1].astype(F32)).astype(BF)
    got_second = place.cross(second, 1)
    own = keep[0].astype(F32) + got[0].astype(F32) + got_second.astype(F32)
    return scatter_line(place, own)


def store_quarters(table, n, depth, row, value, send, keep, vectors=None):
    for pair in range(2):
        flag, slot = table[row * 2 + pair], table[4 + row * 2 + pair]

        def put(ref):
            for line in range(n):
                at = jnp.bitwise_xor(table[8], line)
                data = line * 2 + pair
                ref[slot, at, :depth] = value[data * depth : (data + 1) * depth]
                if vectors is not None:
                    extra = vectors[pl.ds(row * 2 * n + data, 1), :]
                    ref[slot, at, depth:] = jnp.broadcast_to(extra, (EXTRA, extra.shape[1])).astype(BF)

        pl.when(flag == 1)(lambda: put(send))
        pl.when(flag == 0)(lambda: put(keep))


def outer_kernel(n, depth, table, left, right, send, keep):
    width = send.shape[-1]
    for row in range(2):
        value = dot(left[...], right[:, row * width : (row + 1) * width], TN).astype(BF)
        store_quarters(table, n, depth, row, value, send, keep)


def outer(place, table, left, right, depth):
    n, width = place.line_size, right.shape[1] // 2
    if depth % 16:
        halves = [dot(left, right[:, i * width : (i + 1) * width], TN).astype(BF) for i in range(2)]
        return spread(place, jnp.stack(halves), depth)
    shape = ((2, n, depth, width), BF)
    return call(
        functools.partial(outer_kernel, n, depth),
        [shape, shape],
        [table, left, right],
        scalars=1,
        flops=2 * left.size * right.shape[1],
    )


def by_row(value, row, cols):
    kinds = value.shape[1] // (2 * cols)
    return jnp.concatenate(
        [value[:, (2 * t + row) * cols : (2 * t + row + 1) * cols] for t in range(kinds)], axis=1
    )


def outer_attn_kernel(n, depth, cols, table, x, d_qkv, d_att, ctx, vectors, send, keep):
    whole = jnp.concatenate(
        [dot(x[...], d_qkv[...], TN).astype(BF), dot(d_att[...], ctx[...], TN).astype(BF)], axis=1
    )
    for row in range(2):
        store_quarters(table, n, depth, row, by_row(whole, row, cols), send, keep, vectors)


def outer_attn(place, table, x, d_qkv, d_att, ctx, vectors, depth):
    n, cols, width = place.line_size, ctx.shape[1] // 2, x.shape[1]
    if depth % 16:
        whole = jnp.concatenate([dot(x, d_qkv, TN), dot(d_att, ctx, TN)], axis=1).astype(BF)
        return spread(place, jnp.stack([by_row(whole, i, cols) for i in range(2)]), depth, vectors)
    shape = ((2, n, depth + EXTRA, width), BF)
    return call(
        functools.partial(outer_attn_kernel, n, depth, cols),
        [shape, shape],
        [table, x, d_qkv, d_att, ctx, vectors],
        scalars=1,
        flops=2 * x.size * (d_qkv.shape[1] + ctx.shape[1]),
    )


def head_lanes(rows, head):
    lane = lax.broadcasted_iota(jnp.int32, (rows, LANES), 1)
    return (lane < HD) if head == 0 else (lane >= HD)


def attend_kernel(block, chunk, bounds, x, weights, q_bias, v_bias, joined, qkv, probs, ctx, part, mask):
    rows, cols = x.shape[0], q_bias.shape[1]
    half = cols // 2
    for kind in range(4):
        cut = slice(kind * half, (kind + 1) * half)
        joined[:, kind * cols : (kind + 1) * cols] = jnp.concatenate(
            [weights[0, :, cut], weights[1, :, cut]], axis=1
        )

    def labels(index):
        part_of = index // block
        place = index + jnp.where(part_of == 1, block, jnp.where(part_of == 2, -block, 0))
        total = jnp.zeros_like(index)
        for j in range(4):
            total = total + (place >= bounds[j]).astype(jnp.int32)
        return total

    across = labels(lax.broadcasted_iota(jnp.int32, (1, rows), 1))
    down = labels(lax.broadcasted_iota(jnp.int32, (rows, 1), 0))
    mask[...] = jnp.where(down == across, 0.0, -1000000000.0)
    qkv[:, :cols] = (
        (dot(x[...], joined[:, :cols]) + q_bias[...]).astype(BF).astype(F32) * HD ** (-0.5)
    ).astype(BF)
    qkv[:, cols : 2 * cols] = dot(x[...], joined[:, cols : 2 * cols]).astype(BF)
    qkv[:, 2 * cols :] = (dot(x[...], joined[:, 2 * cols : 3 * cols]) + v_bias[...]).astype(BF)

    def pair_step(pair, carry):
        def lanes(kind):
            return pl.ds(pl.multiple_of(kind * cols + pair * LANES, LANES), LANES)

        def row_step(step, inner_carry):
            at = pl.ds(pl.multiple_of(step * chunk, chunk), chunk)
            queries = qkv[at, lanes(0)]
            outs = []
            for head in range(2):
                one = jnp.where(head_lanes(chunk, head), queries, jnp.zeros_like(queries))
                scores = dot(one, qkv[:, lanes(1)], NT) + mask[at, :]
                exponent = jnp.exp(scores - jnp.max(scores, axis=1, keepdims=True))
                low = (exponent * (1.0 / jnp.sum(exponent, axis=1, keepdims=True))).astype(BF)
                probs[pair * 2 + head, at, :] = low
                outs.append(dot(low, qkv[:, lanes(2)]))
            ctx[at, pl.ds(pl.multiple_of(pair * LANES, LANES), LANES)] = jnp.where(
                head_lanes(chunk, 0), outs[0], outs[1]
            ).astype(BF)
            return inner_carry

        return lax.fori_loop(0, rows // chunk, row_step, carry)

    lax.fori_loop(0, cols // LANES, pair_step, 0)
    part[...] = dot(ctx[...], joined[:, 3 * cols :], NT).astype(BF)


def norm_parts(values):
    centred = values - jnp.mean(values, axis=-1, keepdims=True)
    rate = lax.rsqrt(jnp.mean(centred * centred, axis=-1, keepdims=True) + 1e-06)
    return centred * rate, rate


def norm_back(grad, unit, rate, scale):
    inner = grad * scale
    return rate * (
        inner
        - jnp.mean(inner, axis=-1, keepdims=True)
        - unit * jnp.mean(inner * unit, axis=-1, keepdims=True)
    )


def loop_rows(rows, chunk, step):
    def one(index, carry):
        step(pl.ds(pl.multiple_of(index * chunk, chunk), chunk))
        return carry

    lax.fori_loop(0, rows // chunk, one, 0)


def up_kernel(chunk, x, mine, other, norms, up_bias, weights, unit, rate, low, activated, slope, hidden):
    rows, width = x.shape
    units = weights.shape[2]

    def first(at):
        value = x[at, :].astype(F32) + mine[at, :].astype(F32) + other[at, :].astype(F32) + norms[2:3]
        one, scale = norm_parts(value)
        unit[at, :] = one
        rate[at, :] = jnp.broadcast_to(scale, (chunk, LANES))
        low[at, :] = (one * norms[0:1] + norms[3:4]).astype(BF)

    loop_rows(rows, chunk, first)
    for half in range(2):
        cut = slice(half * units, (half + 1) * units)
        hidden[...] = dot(low[...], weights[half])

        def act(at):
            value = hidden[at, :] + up_bias[:, cut]
            share = 0.5 + 0.5 * lax.erf(value * (0.5**0.5))
            activated[at, cut] = (value * share).astype(BF)
            bell = jnp.exp(-0.5 * value * value) * 0.3989422804014327
            slope[at, cut] = (share + value * bell).astype(BF)

        loop_rows(rows, chunk, act)


def down_kernel(activated, weights, part):
    units = weights.shape[2]
    part[...] = (
        dot(activated[:, :units], weights[0], NT) + dot(activated[:, units:], weights[1], NT)
    ).astype(BF)


def column_sums(totals, index, value):
    totals[index : index + 1, :] = totals[index : index + 1, :] + jnp.sum(value, axis=0, keepdims=True)


def second_kernel(chunk, unit, mine, other, grad, norms, result, d_second, d_mixed, totals):
    totals[...] = jnp.zeros_like(totals)

    def step(at):
        normed = unit[at, :] * norms[0:1] + norms[3:4]
        value = normed + mine[at, :].astype(F32) + other[at, :].astype(F32) + norms[4:5]
        one, rate = norm_parts(value)
        result[at, :] = (one * norms[1:2] + norms[5:6]).astype(BF)
        dy = grad[at, :].astype(F32)
        back = norm_back(dy, one, rate, norms[1:2])
        d_second[at, :] = back
        d_mixed[at, :] = back.astype(BF)
        column_sums(totals, 0, dy * one)
        column_sums(totals, 1, back)
        column_sums(totals, 2, dy)

    loop_rows(unit.shape[0], chunk, step)


def hidden_back_kernel(chunk, d_mixed, down, up, slope, d_hidden, part, sums, d_act):
    rows, units = d_mixed.shape[0], down.shape[2]
    sums[...] = jnp.zeros_like(sums)
    for half in range(2):
        cut = slice(half * units, (half + 1) * units)
        d_act[...] = dot(d_mixed[...], down[half])

        def step(at):
            low = (d_act[at, :] * slope[at, cut].astype(F32)).astype(BF)
            d_hidden[at, cut] = low
            sums[0:1, cut] = sums[0:1, cut] + jnp.sum(low.astype(F32), axis=0, keepdims=True)

        loop_rows(rows, chunk, step)
    part[...] = (
        dot(d_hidden[:, :units], up[0], NT) + dot(d_hidden[:, units:], up[1], NT)
    ).astype(BF)


def first_back_kernel(chunk, d_second, mine, other, unit, rate, norms, joined, d_first_in, d_att, d_ctx, totals):
    rows, cols = d_second.shape[0], d_ctx.shape[1]
    totals[...] = jnp.zeros_like(totals)

    def step(at):
        d_first = d_second[at, :] + mine[at, :].astype(F32) + other[at, :].astype(F32)
        one = unit[at, :]
        back = norm_back(d_first, one, rate[at, 0:1], norms[0:1])
        d_first_in[at, :] = back
        d_att[at, :] = back.astype(BF)
        column_sums(totals, 0, d_first * one)
        column_sums(totals, 1, back)
        column_sums(totals, 2, d_first)

    loop_rows(rows, chunk, step)
    d_ctx[...] = dot(d_att[...], joined[:, 3 * cols :]).astype(BF)


def attend_back_kernel(chunk, d_ctx, qkv, probs, ctx, joined, d_qkv, sums, part, d_scores):
    rows, cols = ctx.shape
    sums[...] = jnp.zeros_like(sums)

    def pair_step(pair, carry):
        def lanes(kind):
            return pl.ds(pl.multiple_of(kind * cols + pair * LANES, LANES), LANES)

        def row_step(step, inner_carry):
            at = pl.ds(pl.multiple_of(step * chunk, chunk), chunk)
            grads = d_ctx[at, lanes(0)]
            with_context = grads.astype(F32) * ctx[at, lanes(0)].astype(F32)
            outs = []
            for head in range(2):
                inside = head_lanes(chunk, head)
                one = jnp.where(inside, grads, jnp.zeros_like(grads))
                d_probs = dot(one, qkv[:, lanes(2)], NT)
                inner = jnp.sum(jnp.where(inside, with_context, 0.0), axis=1, keepdims=True)
                low = (probs[pair * 2 + head, at, :].astype(F32) * (d_probs - inner)).astype(BF)
                d_scores[head, at, :] = low
                outs.append(dot(low, qkv[:, lanes(1)]))
            d_queries = (jnp.where(head_lanes(chunk, 0), outs[0], outs[1]) * HD ** (-0.5)).astype(BF)
            d_qkv[at, lanes(0)] = d_queries
            sums[0:1, lanes(0)] = sums[0:1, lanes(0)] + jnp.sum(
                d_queries.astype(F32), axis=0, keepdims=True
            )
            return inner_carry

        lax.fori_loop(0, rows // chunk, row_step, 0)
        d_keys, d_values = 0.0, 0.0
        for head in range(2):
            inside = head_lanes(rows, head)
            queries, grads = qkv[:, lanes(0)], d_ctx[:, lanes(0)]
            d_keys += dot(d_scores[head], jnp.where(inside, queries, jnp.zeros_like(queries)), TN)
            d_values += dot(probs[pair * 2 + head], jnp.where(inside, grads, jnp.zeros_like(grads)), TN)
        d_qkv[:, lanes(1)] = d_keys.astype(BF)
        d_values = d_values.astype(BF)
        d_qkv[:, lanes(2)] = d_values
        sums[0:1, lanes(1)] = jnp.sum(d_values.astype(F32), axis=0, keepdims=True)
        return carry

    lax.fori_loop(0, cols // LANES, pair_step, 0)
    part[...] = dot(d_qkv[...], joined[:, : 3 * cols], NT).astype(BF)


def body(
    inputs, w_qkv, w_out, w_up, w_down, unit_bias, norm_gain, norm_bias, seq_lengths, cotangent
):
    place = Place()
    row, core = place.row, place.core
    groups = place.groups
    block, width = inputs.shape[1], inputs.shape[2]
    rows = 4 * block
    depth, head_cols = w_qkv.shape[1], w_qkv.shape[2]
    units = w_up.shape[1]
    share = unit_bias.shape[1]
    small = norm_gain.shape[1]
    cols = 2 * head_cols
    heads = cols // HD
    chunk = 32

    vector = jnp.concatenate([unit_bias[0], norm_gain.reshape(-1), norm_bias.reshape(-1)])
    vector = jnp.pad(vector[None], ((0, EXTRA - 1), (0, width - vector.shape[0])))
    attn_shard = jnp.concatenate([w_qkv[0], w_qkv[1], w_qkv[2], jnp.transpose(w_out)], axis=1)
    attn_shard = jnp.concatenate([attn_shard, vector], axis=0)
    attn_line = gather_line(place, attn_shard)
    up_shard, attn_line = lax.optimization_barrier((w_up, attn_line))
    up_line = gather_line(place, up_shard)
    down_shard, up_line = lax.optimization_barrier((jnp.transpose(w_down), up_line))
    down_line = gather_line(place, down_shard)

    keep = lambda array, index: lax.dynamic_index_in_dim(array, index, 0, keepdims=False)
    outgoing = jnp.stack([keep(inputs, 1 - row), keep(cotangent, 1 - row)])
    incoming = place.row_swap(outgoing)
    mine = jnp.stack([keep(inputs, row), keep(cotangent, row)])
    low_rows = jnp.where(row == 0, mine, incoming)
    high_rows = jnp.where(row == 0, incoming, mine)
    half = jnp.concatenate([low_rows, high_rows], axis=1)
    other = place.core_swap(half)
    both = jnp.where(
        core == 0,
        jnp.concatenate([half, other], axis=1),
        jnp.concatenate([other, half], axis=1),
    )
    x, grad_rows = both[0], both[1]

    attn_whole, extras = gather_group(place, attn_line, depth)
    up_whole = gather_group(place, up_line, depth)[0]
    down_whole = gather_group(place, down_line, depth)[0]
    vectors = extras[:, :, 0, : share + 6 * small]
    unit_values = vectors[:, :, :share].reshape(2, groups * share).astype(F32)
    norm_here = vectors[:, :, share:]
    norm_there = place.core_swap(norm_here)
    norm_all = jnp.where(
        core == 0,
        jnp.stack([norm_here, norm_there], axis=2),
        jnp.stack([norm_there, norm_here], axis=2),
    )
    norm_all = norm_all.reshape(2, groups, 2, 6, small)
    norm_all = jnp.transpose(norm_all, (3, 1, 0, 2, 4)).reshape(6, width).astype(F32)
    norms = jnp.pad(norm_all, ((0, 2), (0, 0)))
    q_bias = unit_values[:, :head_cols].reshape(1, cols)
    v_bias = unit_values[:, head_cols:cols].reshape(1, cols)
    up_bias = unit_values[:, cols:].reshape(1, 2 * units)
    table = place.scatter_table()

    bounds = jnp.cumsum(keep(seq_lengths, row), dtype=jnp.int32)
    wide = rows * width
    joined, qkv, probs, ctx, part = call(
        functools.partial(attend_kernel, block, 128),
        [
            ((width, 4 * cols), BF),
            ((rows, 3 * cols), BF),
            ((heads, rows, rows), BF),
            ((rows, cols), BF),
            ((rows, width), BF),
        ],
        [bounds, x, attn_whole, q_bias, v_bias],
        scalars=1,
        scratch=[pltpu.VMEM((rows, rows), F32)],
        flops=8 * wide * cols,
    )
    unit, rate, first_low, activated, slope = call(
        functools.partial(up_kernel, chunk),
        [
            ((rows, width), F32),
            ((rows, LANES), F32),
            ((rows, width), BF),
            ((rows, 2 * units), BF),
            ((rows, 2 * units), BF),
        ],
        [x, part, place.core_swap(part), norms, up_bias, up_whole],
        scratch=[pltpu.VMEM((rows, units), F32)],
        flops=4 * wide * units,
    )
    (part,) = call(down_kernel, [((rows, width), BF)], [activated, down_whole], flops=4 * wide * units)
    result, d_second, d_mixed, totals_two = call(
        functools.partial(second_kernel, chunk),
        [((rows, width), BF), ((rows, width), F32), ((rows, width), BF), ((8, width), F32)],
        [unit, part, place.core_swap(part), grad_rows, norms],
        flops=60 * wide,
    )

    down_send, down_keep = outer(place, table, d_mixed, activated, depth)
    grad_down = scatter_group(place, down_send, down_keep)
    d_hidden, part, up_sums = call(
        functools.partial(hidden_back_kernel, chunk),
        [((rows, 2 * units), BF), ((rows, width), BF), ((8, 2 * units), F32)],
        [d_mixed, down_whole, up_whole, slope],
        scratch=[pltpu.VMEM((rows, units), F32)],
        flops=8 * wide * units,
    )
    up_send, up_keep = outer(place, table, first_low, d_hidden, depth)
    grad_up = scatter_group(place, up_send, up_keep)
    d_first_in, d_att, d_ctx, totals_one = call(
        functools.partial(first_back_kernel, chunk),
        [((rows, width), F32), ((rows, width), BF), ((rows, cols), BF), ((8, width), F32)],
        [d_second, part, place.core_swap(part), unit, rate, norms, joined],
        flops=2 * wide * cols,
    )
    d_qkv, attn_sums, part = call(
        functools.partial(attend_back_kernel, 128),
        [((rows, 3 * cols), BF), ((8, 2 * cols), F32), ((rows, width), BF)],
        [d_ctx, qkv, probs, ctx, joined],
        scratch=[pltpu.VMEM((2, rows, rows), BF)],
        flops=10 * wide * cols,
    )
    unit_terms = jnp.concatenate(
        [attn_sums[0, :cols].reshape(2, head_cols), attn_sums[0, cols:].reshape(2, head_cols),
         up_sums[0].reshape(2, units)],
        axis=1,
    ).reshape(2, groups, share)
    norm_terms = jnp.stack(
        [totals_one[0], totals_two[0], totals_one[1], totals_one[2], totals_two[1], totals_two[2]]
    ).reshape(6, groups, 2, 2, small)
    norm_terms = lax.dynamic_index_in_dim(norm_terms, core, 3, keepdims=False)
    norm_terms = jnp.transpose(norm_terms, (2, 1, 0, 3)).reshape(2, groups, 6 * small)
    vector_terms = jnp.concatenate([unit_terms, norm_terms], axis=2)
    vector_terms = jnp.pad(vector_terms, ((0, 0), (0, 0), (0, width - vector_terms.shape[2])))
    attn_send, attn_keep = outer_attn(
        place, table, x, d_qkv, d_att, ctx, vector_terms.reshape(2 * groups, width), depth
    )
    attn_grad = scatter_group(place, attn_send, attn_keep)
    grad_in = d_first_in + part.astype(F32) + place.core_swap(part).astype(F32)

    def hand_back(full):
        mine = lax.dynamic_slice_in_dim(full, core * 2 * block, 2 * block, 0)
        mine = mine.reshape(2, block, width)
        kept = keep(mine, row)
        got = place.row_swap(keep(mine, 1 - row).astype(BF)).astype(full.dtype)
        return jnp.where(row == 0, jnp.stack([kept, got]), jnp.stack([got, kept]))

    grad_qkv = jnp.stack(
        [attn_grad[:depth, t * head_cols : (t + 1) * head_cols] for t in range(3)]
    )
    grad_out = jnp.transpose(attn_grad[:depth, 3 * head_cols :])
    vector_grad = attn_grad[depth]
    norm_grad = vector_grad[share : share + 6 * small].reshape(6, small)
    return (
        hand_back(result),
        hand_back(grad_in),
        grad_qkv,
        grad_out,
        grad_up,
        jnp.transpose(grad_down),
        vector_grad[None, :share],
        norm_grad[:2],
        norm_grad[2:],
    )

def solution(mesh):
    placed = (
        P("dp", "mp", None),
        P(None, "dp", "mp"),
        P("mp", "dp"),
        P("dp", "mp"),
        P("mp", "dp"),
        P("mp", "dp"),
        P(None, ("dp", "mp")),
        P(None, ("dp", "mp")),
        P("dp", None),
        P("dp", "mp", None),
    )
    return jax.shard_map(
        body,
        mesh=mesh,
        in_specs=placed,
        out_specs=(
            P("dp", "mp", None),
            P("dp", "mp", None),
            P(None, "dp", "mp"),
            P("mp", "dp"),
            P("dp", "mp"),
            P("mp", "dp"),
            P("mp", "dp"),
            P(None, ("dp", "mp")),
            P(None, ("dp", "mp")),
        ),
        check_vma=False,
    )
```

```python
import functools

import jax
import jax.numpy as jnp
from jax import lax
from jax.experimental import pallas as pl
from jax.experimental.pallas import tpu as pltpu
from jax.sharding import PartitionSpec as P

HD = 64
LANES = 128
EXTRA = 16
BF = jnp.bfloat16
F32 = jnp.float32
LIMIT = 56 * 1024 * 1024
NN = ((1,), (0,))
NT = ((1,), (1,))
TN = ((0,), (0,))


def dot(left, right, dims=NN):
    return lax.dot_general(left, right, (dims, ((), ())), preferred_element_type=F32)


def call(kernel, outs, args, scalars=0, scratch=(), steps=None):
    args = [arg if isinstance(arg, tuple) else (arg, False) for arg in args]
    outs = [out if len(out) == 3 else out + (False,) for out in outs]

    def spec(shape, cut):
        if steps is None:
            return pl.BlockSpec(memory_space=pltpu.VMEM)
        if cut:
            rest = (0,) * (len(shape) - 1)
            return pl.BlockSpec((shape[0] // steps,) + tuple(shape[1:]), lambda i: (i,) + rest)
        return pl.BlockSpec(tuple(shape), lambda i: (0,) * len(shape))

    return pl.pallas_call(
        kernel,
        out_shape=[jax.ShapeDtypeStruct(shape, kind) for shape, kind, _ in outs],
        grid=() if steps is None else (steps,),
        in_specs=[pl.BlockSpec(memory_space=pltpu.SMEM)] * scalars
        + [spec(arg.shape, cut) for arg, cut in args[scalars:]],
        out_specs=[spec(shape, cut) for shape, _, cut in outs],
        scratch_shapes=list(scratch),
        compiler_params=pltpu.CompilerParams(vmem_limit_bytes=LIMIT),
        cost_estimate=pl.CostEstimate(flops=0, bytes_accessed=0, transcendentals=0),
    )(*[arg for arg, _ in args])


def after(value, *others):
    return lax.optimization_barrier((value,) + others)[0]


class Place:
    def __init__(self):
        self.groups = lax.axis_size("dp")
        self.line_size = self.groups // 2
        data, model = lax.axis_index("dp"), lax.axis_index("mp")
        self.line, self.pair = data // 2, data % 2
        self.row, self.core = model // 2, model % 2

    def core_swap(self, value):
        return lax.ppermute(value, "mp", [(0, 1), (1, 0), (2, 3), (3, 2)])

    def row_swap(self, value):
        return lax.ppermute(value, "mp", [(0, 2), (2, 0), (1, 3), (3, 1)])

    def line_swap(self, value, step):
        pairs = [(i, i ^ (2 * step)) for i in range(self.groups)]
        return lax.ppermute(value, "dp", pairs)

    def cross(self, value, along_row):
        pairs = []
        for data in range(self.groups):
            for model in range(4):
                if model % 2 == along_row:
                    pairs.append((data * 4 + model, data * 4 + (model ^ 2)))
                else:
                    pairs.append((data * 4 + model, (data ^ 1) * 4 + model))
        return lax.ppermute(value, ("dp", "mp"), pairs)

    def quarters(self):
        other_row, other_pair = 1 - self.row, 1 - self.pair
        swap = self.core == 0
        first = (jnp.where(swap, other_row, self.row), jnp.where(swap, self.pair, other_pair))
        second = (jnp.where(swap, self.row, other_row), jnp.where(swap, other_pair, self.pair))
        return (self.row, self.pair), first, second, (other_row, other_pair)

    def roles(self):
        found = []
        for row in range(2):
            for pair in range(2):
                other_row, other_pair = self.row != row, self.pair != pair
                near, far = (other_row, other_pair)
                near = jnp.where(self.core == 0, other_row, other_pair)
                far = jnp.where(self.core == 0, other_pair, other_row)
                found.append(near.astype(jnp.int32) + 2 * far.astype(jnp.int32))
        return jnp.stack(found + [self.line, self.core]).astype(jnp.int32)


def line_parts(place, shard):
    n = place.line_size
    if n <= 4:
        return [shard] + [place.line_swap(shard, step) for step in range(1, n)]
    held, step = shard[None], 1
    while step < n:
        held, step = jnp.concatenate([held, place.line_swap(held, step)]), step * 2
    return [held[i] for i in range(n)]


def scatter_line(place, terms):
    n = place.line_size
    if n <= 4:
        low = terms.astype(BF)
        total = terms[0]
        for step in range(1, n):
            total = total + place.line_swap(low[step], step).astype(F32)
        return total
    step = n // 2
    while step:
        got = place.line_swap(terms[step:].astype(BF), step)
        terms, step = terms[:step] + got.astype(F32), step // 2
    return terms[0]


def place_kernel(depth, n, where, own, first, second, far, whole, extras=None):
    for quarter, source in enumerate((own, first, second, far)):
        row, pair = where[2 * quarter], where[2 * quarter + 1]
        for step in range(n):
            data = jnp.bitwise_xor(where[8], step) * 2 + pair
            start = pl.multiple_of(data * depth, 16)
            whole[row, pl.ds(start, depth), :] = source[step, :depth]
            if extras is not None:
                extras[row, data] = source[step, depth:]


def place_attn_kernel(depth, n, share, where, own, first, second, far, whole, extras, unit):
    place_kernel(depth, n, where, own, first, second, far, whole, extras)
    unit[...] = jnp.zeros_like(unit)
    for row in range(2):
        for data in range(2 * n):
            value = extras[row, data].astype(F32)
            unit[row : row + 1, data * share : (data + 1) * share] = value[0:1, :share]


def place_spots(place):
    spots = [scalar for spot in place.quarters() for scalar in spot] + [place.line]
    return jnp.stack(spots).astype(jnp.int32)


def place_group(place, quarters, depth, share=None):
    n, rows, width = quarters[0].shape
    kind = quarters[0].dtype
    outs = [((2, 2 * n * depth, width), kind)]
    if share is not None:
        outs += [((2, 2 * n, EXTRA, width), kind), ((8, 2 * n * share), F32)]
    if depth % 16 == 0:
        kernel = functools.partial(place_kernel, depth, n)
        if share is not None:
            kernel = functools.partial(place_attn_kernel, depth, n, share)
        return call(kernel, outs, [place_spots(place)] + list(quarters), scalars=1)
    whole = jnp.zeros((2, n, 2, rows, width), kind)
    for piece, (row, pair) in zip(quarters, place.quarters()):
        for step in range(n):
            start = (row, place.line ^ step, pair, 0, 0)
            whole = lax.dynamic_update_slice(whole, piece[step][None, None, None], start)
    out = [whole[:, :, :, :depth].reshape(outs[0][0])]
    if share is not None:
        extras = whole[:, :, :, depth:].reshape(outs[1][0])
        unit = extras[:, :, 0, :share].reshape(2, 2 * n * share).astype(F32)
        out += [extras, jnp.pad(unit, ((0, 6), (0, 0)))]
    return out


def spread(place, terms, depth, vectors=None):
    n = place.line_size
    terms = terms.reshape(2, n, 2, depth, terms.shape[-1])
    if vectors is not None:
        vectors = jnp.pad(vectors, ((0, 0), (0, 0), (0, terms.shape[-1] - vectors.shape[-1])))
        vectors = vectors.reshape(2, n, 2, EXTRA, -1)
        terms = jnp.concatenate([terms, vectors.astype(terms.dtype)], axis=3)
    order = lax.iota(jnp.int32, n) ^ place.line
    terms = jnp.take(terms, order, axis=1)

    def quarter(at):
        size = (1, n, 1) + terms.shape[3:]
        return lax.dynamic_slice(terms, (at[0], 0, at[1], 0, 0), size).reshape((n,) + terms.shape[3:])

    return [quarter(at) for at in place.quarters()]


def store_quarters(table, n, depth, row, value, refs, extra=None):
    for pair in range(2):
        role = table[row * 2 + pair]

        def put(ref):
            for line in range(n):
                at = jnp.bitwise_xor(table[4], line)
                data = line * 2 + pair
                ref[at, :depth] = value[data * depth : (data + 1) * depth]
                if extra is not None:
                    rows = extra(row, data)
                    known = rows.shape[1]
                    ref[at, depth:, :known] = rows
                    ref[at, depth:, known:] = jnp.zeros((EXTRA, ref.shape[2] - known), BF)

        for index in range(4):
            pl.when(role == index)(functools.partial(put, refs[index]))


def outer_kernel(n, depth, table, left, right, *refs):
    width = refs[0].shape[-1]
    turned = left[...].T
    for row in range(2):
        value = dot(turned, right[:, row * width : (row + 1) * width]).astype(BF)
        store_quarters(table, n, depth, row, value, refs)


def outer(place, table, left, right, depth):
    n, width = place.line_size, right.shape[1] // 2
    if depth % 16:
        halves = [dot(left, right[:, i * width : (i + 1) * width], TN).astype(BF) for i in range(2)]
        return spread(place, jnp.stack(halves), depth)
    shape = ((n, depth, width), BF)
    return call(
        functools.partial(outer_kernel, n, depth),
        [shape] * 4,
        [table, left, right],
        scalars=1,
    )


def by_row(value, row, cols):
    kinds = value.shape[1] // (2 * cols)
    return jnp.concatenate(
        [value[:, (2 * t + row) * cols : (2 * t + row + 1) * cols] for t in range(kinds)], axis=1
    )


def vector_rows(groups, cols, units, small, core, attn_sums, up_sums, totals_one, totals_two):
    share = (2 * cols + units) // groups
    known = -(-share // LANES) * LANES
    norms = jnp.concatenate(
        [totals_one[0:1], totals_two[0:1], totals_one[1:3], totals_two[1:3]], axis=0
    )

    def line(row):
        at = slice(row * cols, (row + 1) * cols)
        later = slice((2 + row) * cols, (3 + row) * cols)
        return jnp.concatenate(
            [attn_sums[0:1, at], attn_sums[0:1, later], up_sums[0:1, row * units : (row + 1) * units]], axis=1
        )

    lines = [line(row) for row in range(2)]

    def rows(row, data):
        first = lines[row][:, data * share : (data + 1) * share]
        start = (data * 4 + row * 2) * small
        norm = jnp.where(core == 0, norms[:, start : start + small], norms[:, start + small : start + 2 * small])
        return jnp.concatenate(
            [
                jnp.pad(first, ((0, 0), (0, known - share))),
                jnp.pad(norm, ((0, 0), (0, known - small))),
                jnp.zeros((EXTRA - 7, known), F32),
            ],
            axis=0,
        ).astype(BF)

    return rows


def outer_attn_kernel(n, depth, cols, table, x, d_qkv, d_att, ctx, attn_sums, up_sums, totals_one, totals_two, *refs):
    whole = jnp.concatenate(
        [dot(x[...], d_qkv[...], TN).astype(BF), dot(d_att[...], ctx[...], TN).astype(BF)], axis=1
    )
    units, width = up_sums.shape[1] // 2, x.shape[1]
    extra = vector_rows(
        2 * n, cols, units, width // (8 * n), table[5],
        attn_sums[...], up_sums[...], totals_one[...], totals_two[...],
    )
    for row in range(2):
        store_quarters(table, n, depth, row, by_row(whole, row, cols), refs, extra)


def outer_attn(place, table, x, d_qkv, d_att, ctx, sums, depth):
    n, cols, width = place.line_size, ctx.shape[1] // 2, x.shape[1]
    if depth % 16:
        whole = jnp.concatenate([dot(x, d_qkv, TN), dot(d_att, ctx, TN)], axis=1).astype(BF)
        extra = vector_rows(2 * n, cols, sums[1].shape[1] // 2, width // (8 * n), place.core, *sums)
        vectors = jnp.stack([extra(row, data) for row in range(2) for data in range(2 * n)])
        return spread(place, jnp.stack([by_row(whole, i, cols) for i in range(2)]), depth, vectors)
    shape = ((n, depth + EXTRA, width), BF)
    return call(
        functools.partial(outer_attn_kernel, n, depth, cols),
        [shape] * 4,
        [table, x, d_qkv, d_att, ctx] + list(sums),
        scalars=1,
    )


def head_lanes(rows, head):
    lane = lax.broadcasted_iota(jnp.int32, (rows, LANES), 1)
    return (lane < HD) if head == 0 else (lane >= HD)


def by_kind(unit, start, size):
    return jnp.concatenate([unit[0:1, start : start + size], unit[1:2, start : start + size]], axis=1)


def project_kernel(x, weights, unit, joined, qkv):
    cols = qkv.shape[1] // 3
    half = cols // 2
    for kind in range(4):
        cut = slice(kind * half, (kind + 1) * half)
        joined[:, kind * cols : (kind + 1) * cols] = jnp.concatenate(
            [weights[0, :, cut], weights[1, :, cut]], axis=1
        )
    qkv[:, :cols] = (
        (dot(x[...], joined[:, :cols]) + by_kind(unit, 0, half)).astype(BF).astype(F32) * HD ** (-0.5)
    ).astype(BF)
    qkv[:, cols : 2 * cols] = dot(x[...], joined[:, cols : 2 * cols]).astype(BF)
    qkv[:, 2 * cols :] = (dot(x[...], joined[:, 2 * cols : 3 * cols]) + by_kind(unit, half, half)).astype(BF)


def attend_kernel(block, chunk, bounds, qkv, joined, probs, ctx, part, mask):
    rows, cols = ctx.shape
    pair = pl.program_id(0)

    def labels(index):
        part_of = index // block
        place = index + jnp.where(part_of == 1, block, jnp.where(part_of == 2, -block, 0))
        total = jnp.zeros_like(index)
        for j in range(4):
            total = total + (place >= bounds[j]).astype(jnp.int32)
        return total

    @pl.when(pair == 0)
    def _():
        across = labels(lax.broadcasted_iota(jnp.int32, (1, rows), 1))
        down = labels(lax.broadcasted_iota(jnp.int32, (rows, 1), 0))
        mask[...] = jnp.where(down == across, 0.0, -1000000000.0)

    def lanes(kind):
        return pl.ds(pl.multiple_of(kind * cols + pair * LANES, LANES), LANES)

    keys, values = qkv[:, lanes(1)], qkv[:, lanes(2)]
    for step in range(rows // chunk):
        at = slice(step * chunk, (step + 1) * chunk)
        queries = qkv[at, lanes(0)]
        outs = []
        for head in range(2):
            one = jnp.where(head_lanes(chunk, head), queries, jnp.zeros_like(queries))
            scores = dot(one, keys, NT) + mask[at, :]
            exponent = jnp.exp(scores - jnp.max(scores, axis=1, keepdims=True))
            low = (exponent * (1.0 / jnp.sum(exponent, axis=1, keepdims=True))).astype(BF)
            probs[head, at, :] = low
            outs.append(dot(low, values))
        ctx[at, lanes(0)] = jnp.where(head_lanes(chunk, 0), outs[0], outs[1]).astype(BF)

    @pl.when(pair == pl.num_programs(0) - 1)
    def _():
        part[...] = dot(ctx[...], joined[:, 3 * cols :], NT).astype(BF)


def norm_parts(values):
    centred = values - jnp.mean(values, axis=-1, keepdims=True)
    rate = lax.rsqrt(jnp.mean(centred * centred, axis=-1, keepdims=True) + 1e-06)
    return centred * rate, rate


def norm_back(grad, unit, rate, scale):
    inner = grad * scale
    return rate * (
        inner
        - jnp.mean(inner, axis=-1, keepdims=True)
        - unit * jnp.mean(inner * unit, axis=-1, keepdims=True)
    )


def loop_rows(rows, chunk, step):
    def one(index, carry):
        step(pl.ds(pl.multiple_of(index * chunk, chunk), chunk))
        return carry

    lax.fori_loop(0, rows // chunk, one, 0)


def start_sums(*refs):
    @pl.when(pl.program_id(0) == 0)
    def _():
        for ref in refs:
            ref[...] = jnp.zeros_like(ref)


def up_kernel(chunk, start, x, mine, other, norms, bias, weights, unit, rate, low, activated, slope, hidden):
    rows, units = x.shape[0], weights.shape[2]

    def first(at):
        value = x[at, :].astype(F32) + mine[at, :].astype(F32) + other[at, :].astype(F32) + norms[2:3]
        one, scale = norm_parts(value)
        unit[at, :] = one
        rate[at, :] = jnp.broadcast_to(scale, (chunk, LANES))
        low[at, :] = (one * norms[0:1] + norms[3:4]).astype(BF)

    loop_rows(rows, chunk, first)
    up_bias = by_kind(bias, start, units)
    for half in range(2):
        cut = slice(half * units, (half + 1) * units)
        hidden[...] = dot(low[...], weights[half])

        def act(at):
            value = hidden[at, :] + up_bias[:, cut]
            share = 0.5 + 0.5 * lax.erf(value * (0.5**0.5))
            activated[at, cut] = (value * share).astype(BF)
            bell = jnp.exp(-0.5 * value * value) * 0.3989422804014327
            slope[at, cut] = (share + value * bell).astype(BF)

        loop_rows(rows, chunk, act)


def down_kernel(depth, n, where, activated, own, first, second, far, part, whole):
    pl.when(pl.program_id(0) == 0)(
        lambda: place_kernel(depth, n, where, own, first, second, far, whole)
    )
    units = whole.shape[2]
    part[...] = (
        dot(activated[:, :units], whole[0], NT) + dot(activated[:, units:], whole[1], NT)
    ).astype(BF)


def plain_down_kernel(activated, weights, part):
    units = weights.shape[2]
    part[...] = (
        dot(activated[:, :units], weights[0], NT) + dot(activated[:, units:], weights[1], NT)
    ).astype(BF)


def down(place, activated, quarters, depth):
    n, _, units = quarters[0].shape
    rows, width = activated.shape[0], 2 * n * depth
    if depth % 16:
        weights = place_group(place, quarters, depth)[0]
        part = call(
            plain_down_kernel, [((rows, width), BF, True)], [(activated, True), weights], steps=2
        )[0]
        return part, weights
    return call(
        functools.partial(down_kernel, depth, n),
        [((rows, width), BF, True), ((2, width, units), BF)],
        [place_spots(place), (activated, True)] + list(quarters),
        scalars=1,
        steps=2,
    )


def column_sums(totals, index, value):
    totals[index : index + 1, :] = totals[index : index + 1, :] + jnp.sum(value, axis=0, keepdims=True)


def second_kernel(chunk, unit, mine, other, grad, norms, result, d_second, d_mixed, totals):
    start_sums(totals)

    def step(at):
        normed = unit[at, :] * norms[0:1] + norms[3:4]
        value = normed + mine[at, :].astype(F32) + other[at, :].astype(F32) + norms[4:5]
        one, rate = norm_parts(value)
        result[at, :] = (one * norms[1:2] + norms[5:6]).astype(BF)
        dy = grad[at, :].astype(F32)
        back = norm_back(dy, one, rate, norms[1:2])
        d_second[at, :] = back
        d_mixed[at, :] = back.astype(BF)
        column_sums(totals, 0, dy * one)
        column_sums(totals, 1, back)
        column_sums(totals, 2, dy)

    loop_rows(unit.shape[0], chunk, step)


def hidden_back_kernel(chunk, d_mixed, down, up, slope, d_hidden, part, sums, d_act):
    rows, units = d_mixed.shape[0], down.shape[2]
    start_sums(sums)
    for half in range(2):
        cut = slice(half * units, (half + 1) * units)
        d_act[...] = dot(d_mixed[...], down[half])

        def step(at):
            low = (d_act[at, :] * slope[at, cut].astype(F32)).astype(BF)
            d_hidden[at, cut] = low
            sums[0:1, cut] = sums[0:1, cut] + jnp.sum(low.astype(F32), axis=0, keepdims=True)

        loop_rows(rows, chunk, step)
    part[...] = (
        dot(d_hidden[:, :units], up[0], NT) + dot(d_hidden[:, units:], up[1], NT)
    ).astype(BF)


def first_back_kernel(chunk, d_second, mine, other, unit, rate, norms, joined, d_first_in, d_att, d_ctx, totals):
    rows, cols = d_second.shape[0], d_ctx.shape[1]
    start_sums(totals)

    def step(at):
        d_first = d_second[at, :] + mine[at, :].astype(F32) + other[at, :].astype(F32)
        one = unit[at, :]
        back = norm_back(d_first, one, rate[at, 0:1], norms[0:1])
        d_first_in[at, :] = back
        d_att[at, :] = back.astype(BF)
        column_sums(totals, 0, d_first * one)
        column_sums(totals, 1, back)
        column_sums(totals, 2, d_first)

    loop_rows(rows, chunk, step)
    d_ctx[...] = dot(d_att[...], joined[:, 3 * cols :]).astype(BF)


def attend_back_kernel(chunk, d_ctx, qkv, probs, ctx, d_qkv, sums, d_scores):
    rows, cols = ctx.shape
    pair = pl.program_id(0)
    start_sums(sums)

    def lanes(kind):
        return pl.ds(pl.multiple_of(kind * cols + pair * LANES, LANES), LANES)

    keys, values = qkv[:, lanes(1)], qkv[:, lanes(2)]
    for step in range(rows // chunk):
        at = slice(step * chunk, (step + 1) * chunk)
        grads = d_ctx[at, lanes(0)]
        with_context = grads.astype(F32) * ctx[at, lanes(0)].astype(F32)
        outs = []
        for head in range(2):
            inside = head_lanes(chunk, head)
            one = jnp.where(inside, grads, jnp.zeros_like(grads))
            d_probs = dot(one, values, NT)
            inner = jnp.sum(jnp.where(inside, with_context, 0.0), axis=1, keepdims=True)
            low = (probs[head, at, :].astype(F32) * (d_probs - inner)).astype(BF)
            d_scores[head, at, :] = low
            outs.append(dot(low, keys))
        d_queries = (jnp.where(head_lanes(chunk, 0), outs[0], outs[1]) * HD ** (-0.5)).astype(BF)
        d_qkv[at, lanes(0)] = d_queries
        sums[0:1, lanes(0)] = sums[0:1, lanes(0)] + jnp.sum(
            d_queries.astype(F32), axis=0, keepdims=True
        )
    d_keys, d_values = 0.0, 0.0
    for head in range(2):
        inside = head_lanes(rows, head)
        queries, grads = qkv[:, lanes(0)], d_ctx[:, lanes(0)]
        d_keys += dot(d_scores[head], jnp.where(inside, queries, jnp.zeros_like(queries)), TN)
        d_values += dot(probs[head], jnp.where(inside, grads, jnp.zeros_like(grads)), TN)
    d_qkv[:, lanes(1)] = d_keys.astype(BF)
    d_values = d_values.astype(BF)
    d_qkv[:, lanes(2)] = d_values
    sums[0:1, lanes(1)] = jnp.sum(d_values.astype(F32), axis=0, keepdims=True)


def inputs_kernel(d_qkv, joined, part):
    part[...] = dot(d_qkv[...], joined[:, : d_qkv.shape[1]], NT).astype(BF)


def pack_kernel(w_qkv, w_out_t, unit_bias, norm_gain, norm_bias, attn):
    depth, cols, width = w_qkv.shape[1], w_qkv.shape[2], attn.shape[1]
    for kind in range(3):
        attn[:depth, kind * cols : (kind + 1) * cols] = w_qkv[kind]
    attn[:depth, 3 * cols :] = w_out_t[...]
    small = [ref[...].astype(F32) for ref in (unit_bias, norm_gain, norm_bias)]
    small = [jnp.pad(value, ((0, 0), (0, width - value.shape[1]))) for value in small]
    small.append(jnp.zeros((EXTRA - 7, width), F32))
    attn[depth:, :] = jnp.concatenate(small, axis=0).astype(BF)


def body(
    inputs, w_qkv, w_out, w_up, w_down, unit_bias, norm_gain, norm_bias, seq_lengths, cotangent
):
    place = Place()
    row, core = place.row, place.core
    groups = place.groups
    block, width = inputs.shape[1], inputs.shape[2]
    rows = 4 * block
    depth, head_cols = w_qkv.shape[1], w_qkv.shape[2]
    units = w_up.shape[1]
    share = unit_bias.shape[1]
    small = norm_gain.shape[1]
    cols = 2 * head_cols
    heads = cols // HD
    chunk = 64

    if depth % 16 == 0:
        (attn_shard,) = call(
            pack_kernel,
            [((depth + EXTRA, width), BF)],
            [w_qkv, w_out.T, unit_bias, norm_gain, norm_bias],
        )
    else:
        small_rows = [
            jnp.pad(part, ((0, 0), (0, width - part.shape[1]))) for part in (unit_bias, norm_gain, norm_bias)
        ]
        small_rows.append(jnp.zeros((EXTRA - 7, width), BF))
        attn_shard = jnp.concatenate([w_qkv[0], w_qkv[1], w_qkv[2], w_out.T], axis=1)
        attn_shard = jnp.concatenate([attn_shard] + small_rows, axis=0)
    keep = lambda array, index: lax.dynamic_index_in_dim(array, index, 0, keepdims=False)
    outgoing = jnp.stack([keep(inputs, 1 - row), keep(cotangent, 1 - row)])
    incoming = place.row_swap(outgoing)
    attn_own = jnp.stack(line_parts(place, after(attn_shard, outgoing)))
    attn_own = after(attn_own, incoming)
    attn_first = place.cross(attn_own, 0)
    attn_second = place.cross(attn_own, 1)
    up_parts = line_parts(place, after(w_up, attn_own))
    attn_first = after(attn_first, attn_second)
    attn_far = place.cross(attn_first, 1)
    up_own = jnp.stack([after(part, attn_first) for part in up_parts])
    up_own = after(up_own, attn_far)
    up_first = place.cross(up_own, 0)
    up_second = place.cross(up_own, 1)
    down_parts = line_parts(place, after(w_down.T, up_own))

    mine = jnp.stack([keep(inputs, row), keep(cotangent, row)])
    low_rows = jnp.where(row == 0, mine, incoming)
    high_rows = jnp.where(row == 0, incoming, mine)
    half = jnp.concatenate([low_rows, high_rows], axis=1)
    other = place.core_swap(half)
    both = jnp.where(
        core == 0,
        jnp.concatenate([half, other], axis=1),
        jnp.concatenate([other, half], axis=1),
    )
    x, grad_rows = both[0], both[1]

    attn_whole, extras, unit_bias = place_group(
        place, (attn_own, attn_first, attn_second, attn_far), depth, share
    )
    norm_here = extras[:, :, 1:7, :small]
    norm_there = place.core_swap(norm_here)
    norm_all = jnp.where(
        core == 0,
        jnp.stack([norm_here, norm_there], axis=2),
        jnp.stack([norm_there, norm_here], axis=2),
    )
    norm_all = jnp.transpose(norm_all, (3, 1, 0, 2, 4)).reshape(6, width).astype(F32)
    norms = jnp.pad(norm_all, ((0, 2), (0, 0)))
    table = place.roles()

    bounds = jnp.cumsum(keep(seq_lengths, row), dtype=jnp.int32)
    wide = rows * width
    joined, qkv = call(
        project_kernel,
        [((width, 4 * cols), BF), ((rows, 3 * cols), BF)],
        [x, attn_whole, unit_bias],
    )
    up_first = after(up_first, up_second, qkv)
    up_far = place.cross(up_first, 1)
    down_own = jnp.stack([after(part, up_first) for part in down_parts])
    down_first = place.cross(down_own, 0)
    down_second = place.cross(down_own, 1)
    probs, ctx, part = call(
        functools.partial(attend_kernel, block, 128),
        [((heads, rows, rows), BF, True), ((rows, cols), BF), ((rows, width), BF)],
        [bounds, after(qkv, down_own, norms), joined],
        scalars=1,
        scratch=[pltpu.VMEM((rows, rows), F32)],
        steps=cols // LANES,
    )
    down_first = after(down_first, down_second, ctx)
    down_far = place.cross(down_first, 1)
    up_far = after(up_far, down_first)
    up_whole = place_group(place, (up_own, up_first, up_second, up_far), depth)[0]
    unit, rate, first_low, activated, slope = call(
        functools.partial(up_kernel, chunk, 2 * head_cols),
        [
            ((rows, width), F32, True),
            ((rows, LANES), F32, True),
            ((rows, width), BF, True),
            ((rows, 2 * units), BF, True),
            ((rows, 2 * units), BF, True),
        ],
        [(x, True), (part, True), (place.core_swap(part), True), norms, unit_bias, up_whole],
        scratch=[pltpu.VMEM((rows // 2, units), F32)],
        steps=2,
    )
    part, down_whole = down(place, activated, (down_own, down_first, down_second, down_far), depth)
    result, d_second, d_mixed, totals_two = call(
        functools.partial(second_kernel, chunk),
        [((rows, width), BF, True), ((rows, width), F32, True), ((rows, width), BF, True), ((8, width), F32)],
        [(unit, True), (part, True), (place.core_swap(part), True), (grad_rows, True), norms],
        steps=4,
    )

    down_own, down_first, down_second, down_far = outer(place, table, d_mixed, activated, depth)
    down_got_far = place.cross(down_far, 0)
    d_hidden, part, up_sums = call(
        functools.partial(hidden_back_kernel, chunk),
        [((rows, 2 * units), BF, True), ((rows, width), BF, True), ((8, 2 * units), F32)],
        [(after(d_mixed, down_far), True), down_whole, up_whole, (slope, True)],
        scratch=[pltpu.VMEM((rows // 2, units), F32)],
        steps=2,
    )
    add = lambda one, other: (one.astype(F32) + other.astype(F32)).astype(BF)
    add_three = lambda one, two, three: one.astype(F32) + two.astype(F32) + three.astype(F32)
    down_second = add(down_second, after(down_got_far, d_hidden))
    down_got_second = place.cross(down_second, 1)
    down_got_first = place.cross(after(down_first, down_second), 0)
    up_own, up_first, up_second, up_far = outer(
        place, table, after(first_low, down_second), d_hidden, depth
    )
    up_got_far = place.cross(up_far, 0)
    d_first_in, d_att, d_ctx, totals_one = call(
        functools.partial(first_back_kernel, chunk),
        [((rows, width), F32, True), ((rows, width), BF, True), ((rows, cols), BF, True), ((8, width), F32)],
        [
            (after(d_second, up_far), True),
            (part, True),
            (place.core_swap(part), True),
            (unit, True),
            (rate, True),
            norms,
            joined,
        ],
        steps=4,
    )
    d_qkv, attn_sums = call(
        functools.partial(attend_back_kernel, 128),
        [((rows, 3 * cols), BF), ((8, 2 * cols), F32)],
        [d_ctx, qkv, (probs, True), ctx],
        scratch=[pltpu.VMEM((2, rows, rows), BF)],
        steps=cols // LANES,
    )
    up_second = add(up_second, after(up_got_far, d_qkv))
    up_got_second = place.cross(up_second, 1)
    up_got_first = place.cross(after(up_first, up_second), 0)
    down_sum = add_three(down_own, down_got_first, after(down_got_second, up_second))
    grad_down = scatter_line(place, down_sum)
    attn_own, attn_first, attn_second, attn_far = outer_attn(
        place, table, x, after(d_qkv, up_second, down_sum), d_att, ctx,
        (attn_sums, up_sums, totals_one, totals_two), depth,
    )
    attn_got_far = place.cross(attn_far, 0)
    (part,) = call(
        inputs_kernel,
        [((rows, width), BF, True)],
        [(after(d_qkv, attn_far), True), joined],
        steps=2,
    )
    attn_second = add(attn_second, after(attn_got_far, part))
    attn_got_second = place.cross(attn_second, 1)
    attn_got_first = place.cross(after(attn_first, attn_second), 0)
    up_sum = add_three(up_own, up_got_first, after(up_got_second, attn_second))
    grad_up = scatter_line(place, up_sum)
    grad_in = d_first_in + part.astype(F32) + place.core_swap(part).astype(F32)
    attn_sum = add_three(attn_own, after(attn_got_first, up_sum), attn_got_second)
    attn_grad = scatter_line(place, attn_sum)

    def hand_back(full):
        mine = lax.dynamic_slice_in_dim(full, core * 2 * block, 2 * block, 0)
        mine = mine.reshape(2, block, width)
        kept = keep(mine, row)
        got = place.row_swap(after(keep(mine, 1 - row).astype(BF), attn_sum)).astype(full.dtype)
        return jnp.where(row == 0, jnp.stack([kept, got]), jnp.stack([got, kept]))

    grad_qkv = jnp.stack(
        [attn_grad[:depth, t * head_cols : (t + 1) * head_cols] for t in range(3)]
    )
    grad_out = jnp.transpose(attn_grad[:depth, 3 * head_cols :])
    norm_grad = attn_grad[depth + 1 : depth + 7, :small]
    return (
        hand_back(result),
        hand_back(grad_in),
        grad_qkv,
        grad_out,
        grad_up,
        jnp.transpose(grad_down),
        attn_grad[depth : depth + 1, :share],
        norm_grad[:2],
        norm_grad[2:],
    )

def solution(mesh):
    placed = (
        P("dp", "mp", None),
        P(None, "dp", "mp"),
        P("mp", "dp"),
        P("dp", "mp"),
        P("mp", "dp"),
        P("mp", "dp"),
        P(None, ("dp", "mp")),
        P(None, ("dp", "mp")),
        P("dp", None),
        P("dp", "mp", None),
    )
    return jax.shard_map(
        body,
        mesh=mesh,
        in_specs=placed,
        out_specs=(
            P("dp", "mp", None),
            P("dp", "mp", None),
            P(None, "dp", "mp"),
            P("mp", "dp"),
            P("dp", "mp"),
            P("mp", "dp"),
            P("mp", "dp"),
            P(None, ("dp", "mp")),
            P(None, ("dp", "mp")),
        ),
        check_vma=False,
    )
```

```python
import functools

import jax
import jax.numpy as jnp
from jax import lax
from jax.experimental import pallas as pl
from jax.experimental.pallas import tpu as pltpu
from jax.sharding import PartitionSpec as P

HD = 64
LANES = 128
TILE = 256
EXTRA = 16
BF = jnp.bfloat16
F32 = jnp.float32
LIMIT = 28 * 1024 * 1024
NN = ((1,), (0,))
NT = ((1,), (1,))
TN = ((0,), (0,))


def dot(left, right, dims=NN):
    return lax.dot_general(left, right, (dims, ((), ())), preferred_element_type=F32)


def call(kernel, outs, args, scalars=0, scratch=(), steps=None):
    args = [arg if isinstance(arg, tuple) else (arg, False) for arg in args]
    outs = [out if len(out) == 3 else out + (False,) for out in outs]

    def spec(shape, cut):
        if steps is None:
            return pl.BlockSpec(memory_space=pltpu.VMEM)
        if cut:
            rest = (0,) * (len(shape) - 1)
            return pl.BlockSpec((shape[0] // steps,) + tuple(shape[1:]), lambda i: (i,) + rest)
        return pl.BlockSpec(tuple(shape), lambda i: (0,) * len(shape))

    return pl.pallas_call(
        kernel,
        out_shape=[jax.ShapeDtypeStruct(shape, kind) for shape, kind, _ in outs],
        grid=() if steps is None else (steps,),
        in_specs=[pl.BlockSpec(memory_space=pltpu.SMEM)] * scalars
        + [spec(arg.shape, cut) for arg, cut in args[scalars:]],
        out_specs=[spec(shape, cut) for shape, _, cut in outs],
        scratch_shapes=list(scratch),
        compiler_params=pltpu.CompilerParams(vmem_limit_bytes=LIMIT),
        cost_estimate=pl.CostEstimate(flops=8000000000, bytes_accessed=10000000, transcendentals=0),
    )(*[arg for arg, _ in args])


def after(value, *others):
    return lax.optimization_barrier((value,) + others)[0]


class Place:
    def __init__(self):
        self.groups = lax.axis_size("dp")
        self.line_size = self.groups // 2
        data, model = lax.axis_index("dp"), lax.axis_index("mp")
        self.line, self.pair = data // 2, data % 2
        self.row, self.core = model // 2, model % 2

    def core_swap(self, value):
        return lax.ppermute(value, "mp", [(0, 1), (1, 0), (2, 3), (3, 2)])

    def row_swap(self, value):
        return lax.ppermute(value, "mp", [(0, 2), (2, 0), (1, 3), (3, 1)])

    def line_swap(self, value, step):
        pairs = [(i, i ^ (2 * step)) for i in range(self.groups)]
        return lax.ppermute(value, "dp", pairs)

    def cross(self, value, along_row):
        pairs = []
        for data in range(self.groups):
            for model in range(4):
                if model % 2 == along_row:
                    pairs.append((data * 4 + model, data * 4 + (model ^ 2)))
                else:
                    pairs.append((data * 4 + model, (data ^ 1) * 4 + model))
        return lax.ppermute(value, ("dp", "mp"), pairs)

    def quarters(self):
        other_row, other_pair = 1 - self.row, 1 - self.pair
        swap = self.core == 0
        first = (jnp.where(swap, other_row, self.row), jnp.where(swap, self.pair, other_pair))
        second = (jnp.where(swap, self.row, other_row), jnp.where(swap, other_pair, self.pair))
        return (self.row, self.pair), first, second, (other_row, other_pair)

    def roles(self):
        found = []
        for row in range(2):
            for pair in range(2):
                other_row, other_pair = self.row != row, self.pair != pair
                near, far = (other_row, other_pair)
                near = jnp.where(self.core == 0, other_row, other_pair)
                far = jnp.where(self.core == 0, other_pair, other_row)
                found.append(near.astype(jnp.int32) + 2 * far.astype(jnp.int32))
        return jnp.stack(found + [self.line, self.core]).astype(jnp.int32)


def line_parts(place, shard):
    n = place.line_size
    if n <= 4:
        return [shard] + [place.line_swap(shard, step) for step in range(1, n)]
    held, step = shard[None], 1
    while step < n:
        held, step = jnp.concatenate([held, place.line_swap(held, step)]), step * 2
    return [held[i] for i in range(n)]


def scatter_parts(place, terms):
    n = place.line_size
    if n <= 4:
        low = terms.astype(BF)
        return [place.line_swap(low[step], step) for step in range(1, n)]
    first, step = terms[0], n // 2
    while step:
        got = place.line_swap(terms[step:].astype(BF), step)
        terms, step = terms[:step] + got.astype(F32), step // 2
    return [terms[0] - first]


def total_of(start, parts):
    for part in parts:
        start = start + part.astype(F32)
    return start


def place_kernel(depth, n, where, own, first, second, far, whole, extras=None):
    for quarter, source in enumerate((own, first, second, far)):
        row, pair = where[2 * quarter], where[2 * quarter + 1]
        for step in range(n):
            data = jnp.bitwise_xor(where[8], step) * 2 + pair
            start = pl.multiple_of(data * depth, 16)
            whole[row, pl.ds(start, depth), :] = source[step, :depth]
            if extras is not None:
                extras[row, data] = source[step, depth:]


def place_attn_kernel(depth, n, share, where, own, first, second, far, whole, extras, unit):
    place_kernel(depth, n, where, own, first, second, far, whole, extras)
    unit[...] = jnp.zeros_like(unit)
    for row in range(2):
        for data in range(2 * n):
            value = extras[row, data].astype(F32)
            unit[row : row + 1, data * share : (data + 1) * share] = value[0:1, :share]


def place_spots(place):
    spots = [scalar for spot in place.quarters() for scalar in spot] + [place.line]
    return jnp.stack(spots).astype(jnp.int32)


def place_group(place, quarters, depth, share=None):
    n, rows, width = quarters[0].shape
    kind = quarters[0].dtype
    outs = [((2, 2 * n * depth, width), kind)]
    if share is not None:
        outs += [((2, 2 * n, EXTRA, width), kind), ((8, 2 * n * share), F32)]
    if depth % 16 == 0:
        kernel = functools.partial(place_kernel, depth, n)
        if share is not None:
            kernel = functools.partial(place_attn_kernel, depth, n, share)
        return call(kernel, outs, [place_spots(place)] + list(quarters), scalars=1)
    whole = jnp.zeros((2, n, 2, rows, width), kind)
    for piece, (row, pair) in zip(quarters, place.quarters()):
        for step in range(n):
            start = (row, place.line ^ step, pair, 0, 0)
            whole = lax.dynamic_update_slice(whole, piece[step][None, None, None], start)
    out = [whole[:, :, :, :depth].reshape(outs[0][0])]
    if share is not None:
        extras = whole[:, :, :, depth:].reshape(outs[1][0])
        unit = extras[:, :, 0, :share].reshape(2, 2 * n * share).astype(F32)
        out += [extras, jnp.pad(unit, ((0, 6), (0, 0)))]
    return out


def spread(place, terms, depth, vectors=None):
    n = place.line_size
    terms = terms.reshape(2, n, 2, depth, terms.shape[-1])
    if vectors is not None:
        vectors = jnp.pad(vectors, ((0, 0), (0, 0), (0, terms.shape[-1] - vectors.shape[-1])))
        vectors = vectors.reshape(2, n, 2, EXTRA, -1)
        terms = jnp.concatenate([terms, vectors.astype(terms.dtype)], axis=3)
    order = lax.iota(jnp.int32, n) ^ place.line
    terms = jnp.take(terms, order, axis=1)

    def quarter(at):
        size = (1, n, 1) + terms.shape[3:]
        return lax.dynamic_slice(terms, (at[0], 0, at[1], 0, 0), size).reshape((n,) + terms.shape[3:])

    return [quarter(at) for at in place.quarters()]


def store_quarters(table, n, depth, row, value, refs, extra=None):
    for pair in range(2):
        role = table[row * 2 + pair]

        def put(ref):
            for line in range(n):
                at = jnp.bitwise_xor(table[4], line)
                data = line * 2 + pair
                ref[at, :depth] = value[data * depth : (data + 1) * depth]
                if extra is not None:
                    rows = extra(row, data)
                    known = rows.shape[1]
                    ref[at, depth:, :known] = rows
                    ref[at, depth:, known:] = jnp.zeros((EXTRA, ref.shape[2] - known), BF)

        for index in range(4):
            pl.when(role == index)(functools.partial(put, refs[index]))


def outer_kernel(n, depth, table, left, right, *refs):
    width = refs[0].shape[-1]
    turned = left[...].T
    for row in range(2):
        value = dot(turned, right[:, row * width : (row + 1) * width]).astype(BF)
        store_quarters(table, n, depth, row, value, refs)


def outer(place, table, left, right, depth):
    n, width = place.line_size, right.shape[1] // 2
    if depth % 16:
        halves = [dot(left, right[:, i * width : (i + 1) * width], TN).astype(BF) for i in range(2)]
        return spread(place, jnp.stack(halves), depth)
    shape = ((n, depth, width), BF)
    return call(
        functools.partial(outer_kernel, n, depth),
        [shape] * 4,
        [table, left, right],
        scalars=1,
    )


def by_row(value, row, cols):
    kinds = value.shape[1] // (2 * cols)
    return jnp.concatenate(
        [value[:, (2 * t + row) * cols : (2 * t + row + 1) * cols] for t in range(kinds)], axis=1
    )


def vector_rows(groups, cols, units, small, core, attn_sums, up_sums, totals_one, totals_two):
    share = (2 * cols + units) // groups
    known = -(-share // LANES) * LANES
    norms = jnp.concatenate(
        [totals_one[0:1], totals_two[0:1], totals_one[1:3], totals_two[1:3]], axis=0
    )

    def line(row):
        at = slice(row * cols, (row + 1) * cols)
        later = slice((2 + row) * cols, (3 + row) * cols)
        return jnp.concatenate(
            [attn_sums[0:1, at], attn_sums[0:1, later], up_sums[0:1, row * units : (row + 1) * units]], axis=1
        )

    lines = [line(row) for row in range(2)]

    def rows(row, data):
        first = lines[row][:, data * share : (data + 1) * share]
        start = (data * 4 + row * 2) * small
        norm = jnp.where(core == 0, norms[:, start : start + small], norms[:, start + small : start + 2 * small])
        return jnp.concatenate(
            [
                jnp.pad(first, ((0, 0), (0, known - share))),
                jnp.pad(norm, ((0, 0), (0, known - small))),
                jnp.zeros((EXTRA - 7, known), F32),
            ],
            axis=0,
        ).astype(BF)

    return rows


def outer_attn_kernel(n, depth, cols, table, x, d_qkv, d_att, ctx, attn_sums, up_sums, totals_one, totals_two, *refs):
    whole = jnp.concatenate(
        [dot(x[...], d_qkv[...], TN).astype(BF), dot(d_att[...], ctx[...], TN).astype(BF)], axis=1
    )
    units, width = up_sums.shape[1] // 2, x.shape[1]
    extra = vector_rows(
        2 * n, cols, units, width // (8 * n), table[5],
        attn_sums[...], up_sums[...], totals_one[...], totals_two[...],
    )
    for row in range(2):
        store_quarters(table, n, depth, row, by_row(whole, row, cols), refs, extra)


def outer_attn(place, table, x, d_qkv, d_att, ctx, sums, depth):
    n, cols, width = place.line_size, ctx.shape[1] // 2, x.shape[1]
    if depth % 16:
        whole = jnp.concatenate([dot(x, d_qkv, TN), dot(d_att, ctx, TN)], axis=1).astype(BF)
        extra = vector_rows(2 * n, cols, sums[1].shape[1] // 2, width // (8 * n), place.core, *sums)
        vectors = jnp.stack([extra(row, data) for row in range(2) for data in range(2 * n)])
        return spread(place, jnp.stack([by_row(whole, i, cols) for i in range(2)]), depth, vectors)
    shape = ((n, depth + EXTRA, width), BF)
    return call(
        functools.partial(outer_attn_kernel, n, depth, cols),
        [shape] * 4,
        [table, x, d_qkv, d_att, ctx] + list(sums),
        scalars=1,
    )


def head_lanes(rows, head):
    lane = lax.broadcasted_iota(jnp.int32, (rows, LANES), 1)
    return (lane < HD) if head == 0 else (lane >= HD)


def by_kind(unit, start, size):
    return jnp.concatenate([unit[0:1, start : start + size], unit[1:2, start : start + size]], axis=1)


def project_kernel(x, weights, unit, joined, qkv):
    cols = qkv.shape[1] // 3
    half = cols // 2
    for kind in range(4):
        cut = slice(kind * half, (kind + 1) * half)
        joined[:, kind * cols : (kind + 1) * cols] = jnp.concatenate(
            [weights[0, :, cut], weights[1, :, cut]], axis=1
        )
    qkv[:, :cols] = (
        (dot(x[...], joined[:, :cols]) + by_kind(unit, 0, half)).astype(BF).astype(F32) * HD ** (-0.5)
    ).astype(BF)
    qkv[:, cols : 2 * cols] = dot(x[...], joined[:, cols : 2 * cols]).astype(BF)
    qkv[:, 2 * cols :] = (dot(x[...], joined[:, 2 * cols : 3 * cols]) + by_kind(unit, half, half)).astype(BF)


def attend_kernel(block, chunk, bounds, qkv, joined, probs, ctx, part, mask):
    rows, cols = ctx.shape
    pair = pl.program_id(0)

    def labels(index):
        part_of = index // block
        place = index + jnp.where(part_of == 1, block, jnp.where(part_of == 2, -block, 0))
        total = jnp.zeros_like(index)
        for j in range(4):
            total = total + (place >= bounds[j]).astype(jnp.int32)
        return total

    @pl.when(pair == 0)
    def _():
        across = labels(lax.broadcasted_iota(jnp.int32, (1, rows), 1))
        down = labels(lax.broadcasted_iota(jnp.int32, (rows, 1), 0))
        mask[...] = jnp.where(down == across, 0.0, -1000000000.0)

    def lanes(kind):
        return pl.ds(pl.multiple_of(kind * cols + pair * LANES, LANES), LANES)

    keys, values = qkv[:, lanes(1)], qkv[:, lanes(2)]
    for step in range(rows // chunk):
        at = slice(step * chunk, (step + 1) * chunk)
        queries = qkv[at, lanes(0)]
        heads = [
            jnp.where(head_lanes(chunk, head), queries, jnp.zeros_like(queries)) for head in range(2)
        ]
        scores = [dot(one, keys, NT) + mask[at, :] for one in heads]
        exponents = [jnp.exp(one - jnp.max(one, axis=1, keepdims=True)) for one in scores]
        rates = [1.0 / jnp.sum(one, axis=1, keepdims=True) for one in exponents]
        lows = [(one * rate).astype(BF) for one, rate in zip(exponents, rates)]
        for head in range(2):
            probs[head, at, :] = lows[head]
        outs = [dot(one, values) for one in lows]
        ctx[at, lanes(0)] = jnp.where(head_lanes(chunk, 0), outs[0], outs[1]).astype(BF)

    @pl.when(pair == pl.num_programs(0) - 1)
    def _():
        part[...] = dot(ctx[...], joined[:, 3 * cols :], NT).astype(BF)


def norm_parts(values):
    centred = values - jnp.mean(values, axis=-1, keepdims=True)
    rate = lax.rsqrt(jnp.mean(centred * centred, axis=-1, keepdims=True) + 1e-06)
    return centred * rate, rate


def norm_back(grad, unit, rate, scale):
    inner = grad * scale
    return rate * (
        inner
        - jnp.mean(inner, axis=-1, keepdims=True)
        - unit * jnp.mean(inner * unit, axis=-1, keepdims=True)
    )


def start_sums(*refs):
    @pl.when(pl.program_id(0) == 0)
    def _():
        for ref in refs:
            ref[...] = jnp.zeros_like(ref)


def up_kernel(start, x, mine, other, norms, bias, weights, unit, rate, low, activated, slope):
    units = weights.shape[2]
    first_in = x[...].astype(F32) + mine[...].astype(F32) + other[...].astype(F32) + norms[2:3]
    one, scale = norm_parts(first_in)
    unit[...] = one.astype(BF)
    rate[...] = jnp.broadcast_to(scale, rate.shape)
    normed = (one * norms[0:1] + norms[3:4]).astype(BF)
    low[...] = normed
    up_bias = by_kind(bias, start, units)
    for half in range(2):
        for part in range(units // TILE):
            cut = slice(half * units + part * TILE, half * units + (part + 1) * TILE)
            value = dot(normed, weights[half, :, part * TILE : (part + 1) * TILE]) + up_bias[:, cut]
            share = 0.5 + 0.5 * lax.erf(value * (0.5**0.5))
            activated[:, cut] = (value * share).astype(BF)
            bell = jnp.exp(-0.5 * value * value) * 0.3989422804014327
            slope[:, cut] = (share + value * bell).astype(BF)


def down_kernel(depth, n, where, activated, own, first, second, far, part, whole):
    pl.when(pl.program_id(0) == 0)(
        lambda: place_kernel(depth, n, where, own, first, second, far, whole)
    )
    units = whole.shape[2]
    part[...] = (
        dot(activated[:, :units], whole[0], NT) + dot(activated[:, units:], whole[1], NT)
    ).astype(BF)


def plain_down_kernel(activated, weights, part):
    units = weights.shape[2]
    part[...] = (
        dot(activated[:, :units], weights[0], NT) + dot(activated[:, units:], weights[1], NT)
    ).astype(BF)


def down(place, activated, quarters, depth):
    n, _, units = quarters[0].shape
    rows, width = activated.shape[0], 2 * n * depth
    if depth % 16:
        weights = place_group(place, quarters, depth)[0]
        part = call(
            plain_down_kernel, [((rows, width), BF, True)], [(activated, True), weights], steps=2
        )[0]
        return part, weights
    return call(
        functools.partial(down_kernel, depth, n),
        [((rows, width), BF, True), ((2, width, units), BF)],
        [place_spots(place), (activated, True)] + list(quarters),
        scalars=1,
        steps=2,
    )


def column_sums(totals, index, value):
    totals[index : index + 1, :] = totals[index : index + 1, :] + jnp.sum(value, axis=0, keepdims=True)


def second_kernel(unit, mine, other, grad, norms, result, d_mixed, totals):
    start_sums(totals)
    normed = unit[...].astype(F32) * norms[0:1] + norms[3:4]
    one, rate = norm_parts(normed + mine[...].astype(F32) + other[...].astype(F32) + norms[4:5])
    result[...] = (one * norms[1:2] + norms[5:6]).astype(BF)
    dy = grad[...].astype(F32)
    back = norm_back(dy, one, rate, norms[1:2])
    d_mixed[...] = back.astype(BF)
    column_sums(totals, 0, dy * one)
    column_sums(totals, 1, back)
    column_sums(totals, 2, dy)


def hidden_back_kernel(d_mixed, down, up, slope, d_hidden, part, sums):
    units = down.shape[2]
    start_sums(sums)
    total = 0.0
    for half in range(2):
        cut = slice(half * units, (half + 1) * units)
        low = (dot(d_mixed[...], down[half]) * slope[:, cut].astype(F32)).astype(BF)
        d_hidden[:, cut] = low
        sums[0:1, cut] = sums[0:1, cut] + jnp.sum(low.astype(F32), axis=0, keepdims=True)
        total += dot(low, up[half], NT)
    part[...] = total.astype(BF)


def first_back_kernel(d_second, mine, other, unit, rate, norms, joined, d_att, d_ctx, totals):
    cols = d_ctx.shape[1]
    start_sums(totals)
    d_first = d_second[...].astype(F32) + mine[...].astype(F32) + other[...].astype(F32)
    one = unit[...].astype(F32)
    back = norm_back(d_first, one, rate[:, 0:1], norms[0:1])
    low = back.astype(BF)
    d_att[...] = low
    column_sums(totals, 0, d_first * one)
    column_sums(totals, 1, back)
    column_sums(totals, 2, d_first)
    d_ctx[...] = dot(low, joined[:, 3 * cols :]).astype(BF)


def attend_back_kernel(chunk, d_ctx, qkv, probs, ctx, d_qkv, sums, d_scores):
    rows, cols = ctx.shape
    pair = pl.program_id(0)
    start_sums(sums)

    def lanes(kind):
        return pl.ds(pl.multiple_of(kind * cols + pair * LANES, LANES), LANES)

    keys, values = qkv[:, lanes(1)], qkv[:, lanes(2)]
    for step in range(rows // chunk):
        at = slice(step * chunk, (step + 1) * chunk)
        grads = d_ctx[at, lanes(0)]
        with_context = grads.astype(F32) * ctx[at, lanes(0)].astype(F32)
        inside = [head_lanes(chunk, head) for head in range(2)]
        ones = [jnp.where(lane, grads, jnp.zeros_like(grads)) for lane in inside]
        d_probs = [dot(one, values, NT) for one in ones]
        inner = [jnp.sum(jnp.where(lane, with_context, 0.0), axis=1, keepdims=True) for lane in inside]
        lows = [
            (probs[head, at, :].astype(F32) * (d_probs[head] - inner[head])).astype(BF)
            for head in range(2)
        ]
        for head in range(2):
            d_scores[head, at, :] = lows[head]
        outs = [dot(one, keys) for one in lows]
        d_queries = (jnp.where(head_lanes(chunk, 0), outs[0], outs[1]) * HD ** (-0.5)).astype(BF)
        d_qkv[at, lanes(0)] = d_queries
        sums[0:1, lanes(0)] = sums[0:1, lanes(0)] + jnp.sum(
            d_queries.astype(F32), axis=0, keepdims=True
        )
    d_keys, d_values = 0.0, 0.0
    for head in range(2):
        inside = head_lanes(rows, head)
        queries, grads = qkv[:, lanes(0)], d_ctx[:, lanes(0)]
        d_keys += dot(d_scores[head], jnp.where(inside, queries, jnp.zeros_like(queries)), TN)
        d_values += dot(probs[head], jnp.where(inside, grads, jnp.zeros_like(grads)), TN)
    d_qkv[:, lanes(1)] = d_keys.astype(BF)
    d_values = d_values.astype(BF)
    d_qkv[:, lanes(2)] = d_values
    sums[0:1, lanes(1)] = jnp.sum(d_values.astype(F32), axis=0, keepdims=True)


def inputs_kernel(d_qkv, joined, part):
    part[...] = dot(d_qkv[...], joined[:, : d_qkv.shape[1]], NT).astype(BF)


def pack_kernel(w_qkv, w_out_t, unit_bias, norm_gain, norm_bias, attn):
    depth, cols, width = w_qkv.shape[1], w_qkv.shape[2], attn.shape[1]
    for kind in range(3):
        attn[:depth, kind * cols : (kind + 1) * cols] = w_qkv[kind]
    attn[:depth, 3 * cols :] = w_out_t[...]
    small = [ref[...].astype(F32) for ref in (unit_bias, norm_gain, norm_bias)]
    small = [jnp.pad(value, ((0, 0), (0, width - value.shape[1]))) for value in small]
    small.append(jnp.zeros((EXTRA - 7, width), F32))
    attn[depth:, :] = jnp.concatenate(small, axis=0).astype(BF)


def body(
    inputs, w_qkv, w_out, w_up, w_down, unit_bias, norm_gain, norm_bias, seq_lengths, cotangent
):
    place = Place()
    row, core = place.row, place.core
    groups = place.groups
    block, width = inputs.shape[1], inputs.shape[2]
    rows = 4 * block
    depth, head_cols = w_qkv.shape[1], w_qkv.shape[2]
    units = w_up.shape[1]
    share = unit_bias.shape[1]
    small = norm_gain.shape[1]
    cols = 2 * head_cols
    heads = cols // HD

    if depth % 16 == 0:
        (attn_shard,) = call(
            pack_kernel,
            [((depth + EXTRA, width), BF)],
            [w_qkv, w_out.T, unit_bias, norm_gain, norm_bias],
        )
    else:
        small_rows = [
            jnp.pad(part, ((0, 0), (0, width - part.shape[1]))) for part in (unit_bias, norm_gain, norm_bias)
        ]
        small_rows.append(jnp.zeros((EXTRA - 7, width), BF))
        attn_shard = jnp.concatenate([w_qkv[0], w_qkv[1], w_qkv[2], w_out.T], axis=1)
        attn_shard = jnp.concatenate([attn_shard] + small_rows, axis=0)
    keep = lambda array, index: lax.dynamic_index_in_dim(array, index, 0, keepdims=False)
    outgoing = jnp.stack([keep(inputs, 1 - row), keep(cotangent, 1 - row)])
    incoming = place.row_swap(outgoing)
    attn_own = jnp.stack(line_parts(place, after(attn_shard, outgoing)))
    attn_own = after(attn_own, incoming)
    attn_first, attn_second = place.cross(attn_own, 0), place.cross(attn_own, 1)
    up_own = jnp.stack(line_parts(place, after(w_up, attn_own)))
    attn_first = after(attn_first, attn_second, up_own)
    attn_far = place.cross(attn_first, 1)
    up_own = after(up_own, attn_first)
    up_first, up_second = place.cross(up_own, 0), place.cross(up_own, 1)
    down_own = jnp.stack(line_parts(place, after(w_down.T, up_own)))

    mine = jnp.stack([keep(inputs, row), keep(cotangent, row)])
    low_rows = jnp.where(row == 0, mine, incoming)
    high_rows = jnp.where(row == 0, incoming, mine)
    half = jnp.concatenate([low_rows, high_rows], axis=1)
    other = place.core_swap(half)
    both = jnp.where(
        core == 0,
        jnp.concatenate([half, other], axis=1),
        jnp.concatenate([other, half], axis=1),
    )
    x, grad_rows = both[0], both[1]

    attn_whole, extras, unit_bias = place_group(
        place, (attn_own, attn_first, attn_second, attn_far), depth, share
    )
    norm_here = extras[:, :, 1:7, :small]
    norm_there = place.core_swap(norm_here)
    norm_all = jnp.where(
        core == 0,
        jnp.stack([norm_here, norm_there], axis=2),
        jnp.stack([norm_there, norm_here], axis=2),
    )
    norm_all = jnp.transpose(norm_all, (3, 1, 0, 2, 4)).reshape(6, width).astype(F32)
    norms = jnp.pad(norm_all, ((0, 2), (0, 0)))
    table = place.roles()

    bounds = jnp.cumsum(keep(seq_lengths, row), dtype=jnp.int32)
    wide = rows * width
    joined, qkv = call(
        project_kernel,
        [((width, 4 * cols), BF), ((rows, 3 * cols), BF)],
        [x, attn_whole, unit_bias],
    )
    up_first = after(up_first, up_second, down_own, qkv)
    up_far = place.cross(up_first, 1)
    down_own = after(down_own, up_first)
    down_first, down_second = place.cross(down_own, 0), place.cross(down_own, 1)
    probs, ctx, part = call(
        functools.partial(attend_kernel, block, rows),
        [((heads, rows, rows), BF, True), ((rows, cols), BF), ((rows, width), BF)],
        [bounds, after(qkv, up_first, norms), joined],
        scalars=1,
        scratch=[pltpu.VMEM((rows, rows), F32)],
        steps=cols // LANES,
    )
    down_first = after(down_first, down_second, ctx)
    down_far = place.cross(down_first, 1)
    up_far = after(up_far, down_first)
    up_whole = place_group(place, (up_own, up_first, up_second, up_far), depth)[0]
    unit, rate, first_low, activated, slope = call(
        functools.partial(up_kernel, 2 * head_cols),
        [
            ((rows, width), BF, True),
            ((rows, LANES), F32, True),
            ((rows, width), BF, True),
            ((rows, 2 * units), BF, True),
            ((rows, 2 * units), BF, True),
        ],
        [(x, True), (part, True), (place.core_swap(part), True), norms, unit_bias, up_whole],
        steps=2,
    )
    part, down_whole = down(place, activated, (down_own, down_first, down_second, down_far), depth)
    result, d_mixed, totals_two = call(
        second_kernel,
        [((rows, width), BF, True), ((rows, width), BF, True), ((8, width), F32)],
        [(unit, True), (part, True), (place.core_swap(part), True), (grad_rows, True), norms],
        steps=2,
    )

    down_own, down_first, down_second, down_far = outer(place, table, d_mixed, activated, depth)
    down_got_far = place.cross(down_far, 0)
    d_hidden, part, up_sums = call(
        hidden_back_kernel,
        [((rows, 2 * units), BF, True), ((rows, width), BF, True), ((8, 2 * units), F32)],
        [(after(d_mixed, down_far), True), down_whole, up_whole, (slope, True)],
        steps=2,
    )
    add = lambda one, other: (one.astype(F32) + other.astype(F32)).astype(BF)
    add_three = lambda one, two, three: one.astype(F32) + two.astype(F32) + three.astype(F32)
    up_own, up_first, up_second, up_far = outer(place, table, first_low, d_hidden, depth)
    down_second = add(down_second, after(down_got_far, up_far))
    down_got_second = place.cross(down_second, 1)
    down_got_first = place.cross(after(down_first, down_far), 0)
    up_got_far = place.cross(after(up_far, down_second), 0)
    d_att, d_ctx, totals_one = call(
        first_back_kernel,
        [((rows, width), BF, True), ((rows, cols), BF, True), ((8, width), F32)],
        [
            (after(d_mixed, down_second), True),
            (part, True),
            (place.core_swap(part), True),
            (unit, True),
            (rate, True),
            norms,
            joined,
        ],
        steps=2,
    )
    d_qkv, attn_sums = call(
        functools.partial(attend_back_kernel, rows),
        [((rows, 3 * cols), BF), ((8, 2 * cols), F32)],
        [d_ctx, qkv, (probs, True), ctx],
        scratch=[pltpu.VMEM((2, rows, rows), BF)],
        steps=cols // LANES,
    )
    attn_own, attn_first, attn_second, attn_far = outer_attn(
        place, table, x, d_qkv, d_att, ctx,
        (attn_sums, up_sums, totals_one, totals_two), depth,
    )
    attn_got_far = place.cross(attn_far, 0)
    up_second = add(up_second, after(up_got_far, attn_far))
    up_got_second = place.cross(up_second, 1)
    up_got_first = place.cross(after(up_first, up_second), 0)
    down_sum = add_three(down_own, down_got_first, after(down_got_second, up_second))
    down_parts = scatter_parts(place, down_sum)
    (part,) = call(
        inputs_kernel,
        [((rows, width), BF, True)],
        [(after(d_qkv, down_sum), True), joined],
        steps=2,
    )
    grad_in = d_att.astype(F32) + part.astype(F32) + place.core_swap(part).astype(F32)
    attn_second = add(attn_second, after(attn_got_far, part))
    attn_got_second = place.cross(attn_second, 1)
    attn_got_first = place.cross(after(attn_first, attn_second), 0)
    grad_down = total_of(down_sum[0], down_parts)
    up_sum = add_three(up_own, up_got_first, after(up_got_second, attn_second))
    up_parts = scatter_parts(place, up_sum)
    attn_sum = add_three(attn_own, after(attn_got_first, *down_parts, *up_parts), attn_got_second)
    attn_grad = total_of(attn_sum[0], scatter_parts(place, attn_sum))
    grad_up = total_of(up_sum[0], up_parts)

    def hand_back(full):
        mine = lax.dynamic_slice_in_dim(full, core * 2 * block, 2 * block, 0)
        mine = mine.reshape(2, block, width)
        kept = keep(mine, row)
        got = place.row_swap(after(keep(mine, 1 - row).astype(BF), attn_sum)).astype(full.dtype)
        return jnp.where(row == 0, jnp.stack([kept, got]), jnp.stack([got, kept]))

    grad_qkv = jnp.stack(
        [attn_grad[:depth, t * head_cols : (t + 1) * head_cols] for t in range(3)]
    )
    grad_out = jnp.transpose(attn_grad[:depth, 3 * head_cols :])
    norm_grad = attn_grad[depth + 1 : depth + 7, :small]
    return (
        hand_back(result),
        hand_back(grad_in),
        grad_qkv,
        grad_out,
        grad_up,
        jnp.transpose(grad_down),
        attn_grad[depth : depth + 1, :share],
        norm_grad[:2],
        norm_grad[2:],
    )

def solution(mesh):
    placed = (
        P("dp", "mp", None),
        P(None, "dp", "mp"),
        P("mp", "dp"),
        P("dp", "mp"),
        P("mp", "dp"),
        P("mp", "dp"),
        P(None, ("dp", "mp")),
        P(None, ("dp", "mp")),
        P("dp", None),
        P("dp", "mp", None),
    )
    return jax.shard_map(
        body,
        mesh=mesh,
        in_specs=placed,
        out_specs=(
            P("dp", "mp", None),
            P("dp", "mp", None),
            P(None, "dp", "mp"),
            P("mp", "dp"),
            P("dp", "mp"),
            P("mp", "dp"),
            P("mp", "dp"),
            P(None, ("dp", "mp")),
            P(None, ("dp", "mp")),
        ),
        check_vma=False,
    )
```

```python
import functools

import jax
import jax.numpy as jnp
from jax import lax
from jax.experimental import pallas as pl
from jax.experimental.pallas import tpu as pltpu
from jax.sharding import PartitionSpec as P

HD = 64
LANES = 128
TILE = 256
EXTRA = 16
BF = jnp.bfloat16
F32 = jnp.float32
LIMIT = 28 * 1024 * 1024
NN = ((1,), (0,))
NT = ((1,), (1,))
TN = ((0,), (0,))


def dot(left, right, dims=NN):
    return lax.dot_general(left, right, (dims, ((), ())), preferred_element_type=F32)


def call(kernel, outs, args, scalars=0, scratch=(), steps=None):
    args = [arg if isinstance(arg, tuple) else (arg, False) for arg in args]
    outs = [out if len(out) == 3 else out + (False,) for out in outs]

    def spec(shape, cut):
        if steps is None:
            return pl.BlockSpec(memory_space=pltpu.VMEM)
        if cut:
            rest = (0,) * (len(shape) - 1)
            return pl.BlockSpec((shape[0] // steps,) + tuple(shape[1:]), lambda i: (i,) + rest)
        return pl.BlockSpec(tuple(shape), lambda i: (0,) * len(shape))

    return pl.pallas_call(
        kernel,
        out_shape=[jax.ShapeDtypeStruct(shape, kind) for shape, kind, _ in outs],
        grid=() if steps is None else (steps,),
        in_specs=[pl.BlockSpec(memory_space=pltpu.SMEM)] * scalars
        + [spec(arg.shape, cut) for arg, cut in args[scalars:]],
        out_specs=[spec(shape, cut) for shape, _, cut in outs],
        scratch_shapes=list(scratch),
        compiler_params=pltpu.CompilerParams(vmem_limit_bytes=LIMIT),
        cost_estimate=pl.CostEstimate(flops=8000000000, bytes_accessed=10000000, transcendentals=0),
    )(*[arg for arg, _ in args])


def after(value, *others):
    return lax.optimization_barrier((value,) + others)[0]


class Place:
    def __init__(self):
        self.groups = lax.axis_size("dp")
        self.line_size = self.groups // 2
        data, model = lax.axis_index("dp"), lax.axis_index("mp")
        self.line, self.pair = data // 2, data % 2
        self.row, self.core = model // 2, model % 2

    def core_swap(self, value):
        return lax.ppermute(value, "mp", [(0, 1), (1, 0), (2, 3), (3, 2)])

    def row_swap(self, value):
        return lax.ppermute(value, "mp", [(0, 2), (2, 0), (1, 3), (3, 1)])

    def line_swap(self, value, step):
        pairs = [(i, i ^ (2 * step)) for i in range(self.groups)]
        return lax.ppermute(value, "dp", pairs)

    def cross(self, value, along_row):
        pairs = []
        for data in range(self.groups):
            for model in range(4):
                if model % 2 == along_row:
                    pairs.append((data * 4 + model, data * 4 + (model ^ 2)))
                else:
                    pairs.append((data * 4 + model, (data ^ 1) * 4 + model))
        return lax.ppermute(value, ("dp", "mp"), pairs)

    def quarters(self):
        other_row, other_pair = 1 - self.row, 1 - self.pair
        swap = self.core == 0
        first = (jnp.where(swap, other_row, self.row), jnp.where(swap, self.pair, other_pair))
        second = (jnp.where(swap, self.row, other_row), jnp.where(swap, other_pair, self.pair))
        return (self.row, self.pair), first, second, (other_row, other_pair)

    def roles(self):
        found = []
        for row in range(2):
            for pair in range(2):
                other_row, other_pair = self.row != row, self.pair != pair
                near, far = (other_row, other_pair)
                near = jnp.where(self.core == 0, other_row, other_pair)
                far = jnp.where(self.core == 0, other_pair, other_row)
                found.append(near.astype(jnp.int32) + 2 * far.astype(jnp.int32))
        return jnp.stack(found + [self.line, self.core]).astype(jnp.int32)


def line_parts(place, shard):
    n = place.line_size
    if n <= 4:
        return [shard] + [place.line_swap(shard, step) for step in range(1, n)]
    held, step = shard[None], 1
    while step < n:
        held, step = jnp.concatenate([held, place.line_swap(held, step)]), step * 2
    return [held[i] for i in range(n)]


def scatter_parts(place, terms):
    n = place.line_size
    if n <= 4:
        low = terms.astype(BF)
        return [place.line_swap(low[step], step) for step in range(1, n)]
    first, step = terms[0], n // 2
    while step:
        got = place.line_swap(terms[step:].astype(BF), step)
        terms, step = terms[:step] + got.astype(F32), step // 2
    return [terms[0] - first]


def total_of(start, parts):
    for part in parts:
        start = start + part.astype(F32)
    return start


def place_kernel(depth, n, where, own, first, second, far, whole, extras=None):
    for quarter, source in enumerate((own, first, second, far)):
        row, pair = where[2 * quarter], where[2 * quarter + 1]
        for step in range(n):
            data = jnp.bitwise_xor(where[8], step) * 2 + pair
            start = pl.multiple_of(data * depth, 16)
            whole[row, pl.ds(start, depth), :] = source[step, :depth]
            if extras is not None:
                extras[row, data] = source[step, depth:]


def place_attn_kernel(depth, n, share, where, own, first, second, far, whole, extras, unit):
    place_kernel(depth, n, where, own, first, second, far, whole, extras)
    unit[...] = jnp.zeros_like(unit)
    for row in range(2):
        for data in range(2 * n):
            value = extras[row, data].astype(F32)
            unit[row : row + 1, data * share : (data + 1) * share] = value[0:1, :share]


def place_spots(place):
    spots = [scalar for spot in place.quarters() for scalar in spot] + [place.line]
    return jnp.stack(spots).astype(jnp.int32)


def place_group(place, quarters, depth, share=None):
    n, rows, width = quarters[0].shape
    kind = quarters[0].dtype
    outs = [((2, 2 * n * depth, width), kind)]
    if share is not None:
        outs += [((2, 2 * n, EXTRA, width), kind), ((8, 2 * n * share), F32)]
    if depth % 16 == 0:
        kernel = functools.partial(place_kernel, depth, n)
        if share is not None:
            kernel = functools.partial(place_attn_kernel, depth, n, share)
        return call(kernel, outs, [place_spots(place)] + list(quarters), scalars=1)
    whole = jnp.zeros((2, n, 2, rows, width), kind)
    for piece, (row, pair) in zip(quarters, place.quarters()):
        for step in range(n):
            start = (row, place.line ^ step, pair, 0, 0)
            whole = lax.dynamic_update_slice(whole, piece[step][None, None, None], start)
    out = [whole[:, :, :, :depth].reshape(outs[0][0])]
    if share is not None:
        extras = whole[:, :, :, depth:].reshape(outs[1][0])
        unit = extras[:, :, 0, :share].reshape(2, 2 * n * share).astype(F32)
        out += [extras, jnp.pad(unit, ((0, 6), (0, 0)))]
    return out


def spread(place, terms, depth, vectors=None):
    n = place.line_size
    terms = terms.reshape(2, n, 2, depth, terms.shape[-1])
    if vectors is not None:
        vectors = jnp.pad(vectors, ((0, 0), (0, 0), (0, terms.shape[-1] - vectors.shape[-1])))
        vectors = vectors.reshape(2, n, 2, EXTRA, -1)
        terms = jnp.concatenate([terms, vectors.astype(terms.dtype)], axis=3)
    order = lax.iota(jnp.int32, n) ^ place.line
    terms = jnp.take(terms, order, axis=1)

    def quarter(at):
        size = (1, n, 1) + terms.shape[3:]
        return lax.dynamic_slice(terms, (at[0], 0, at[1], 0, 0), size).reshape((n,) + terms.shape[3:])

    return [quarter(at) for at in place.quarters()]


def store_quarters(table, n, depth, row, value, refs, extra=None):
    for pair in range(2):
        role = table[row * 2 + pair]

        def put(ref):
            for line in range(n):
                at = jnp.bitwise_xor(table[4], line)
                data = line * 2 + pair
                ref[at, :depth] = value[data * depth : (data + 1) * depth]
                if extra is not None:
                    rows = extra(row, data)
                    known = rows.shape[1]
                    ref[at, depth:, :known] = rows
                    ref[at, depth:, known:] = jnp.zeros((EXTRA, ref.shape[2] - known), BF)

        for index in range(4):
            pl.when(role == index)(functools.partial(put, refs[index]))


def outer_kernel(n, depth, table, left, right, *refs):
    width = refs[0].shape[-1]
    turned = left[...].T
    for row in range(2):
        value = dot(turned, right[:, row * width : (row + 1) * width]).astype(BF)
        store_quarters(table, n, depth, row, value, refs)


def outer(place, table, left, right, depth):
    n, width = place.line_size, right.shape[1] // 2
    if depth % 16:
        halves = [dot(left, right[:, i * width : (i + 1) * width], TN).astype(BF) for i in range(2)]
        return spread(place, jnp.stack(halves), depth)
    shape = ((n, depth, width), BF)
    return call(
        functools.partial(outer_kernel, n, depth),
        [shape] * 4,
        [table, left, right],
        scalars=1,
    )


def by_row(value, row, cols):
    kinds = value.shape[1] // (2 * cols)
    return jnp.concatenate(
        [value[:, (2 * t + row) * cols : (2 * t + row + 1) * cols] for t in range(kinds)], axis=1
    )


def vector_rows(groups, cols, units, small, core, attn_sums, up_sums, totals_one, totals_two):
    share = (2 * cols + units) // groups
    known = -(-share // LANES) * LANES
    norms = jnp.concatenate(
        [totals_one[0:1], totals_two[0:1], totals_one[1:3], totals_two[1:3]], axis=0
    )

    def line(row):
        at = slice(row * cols, (row + 1) * cols)
        later = slice((2 + row) * cols, (3 + row) * cols)
        return jnp.concatenate(
            [attn_sums[0:1, at], attn_sums[0:1, later], up_sums[0:1, row * units : (row + 1) * units]], axis=1
        )

    lines = [line(row) for row in range(2)]

    def rows(row, data):
        first = lines[row][:, data * share : (data + 1) * share]
        start = (data * 4 + row * 2) * small
        norm = jnp.where(core == 0, norms[:, start : start + small], norms[:, start + small : start + 2 * small])
        return jnp.concatenate(
            [
                jnp.pad(first, ((0, 0), (0, known - share))),
                jnp.pad(norm, ((0, 0), (0, known - small))),
                jnp.zeros((EXTRA - 7, known), F32),
            ],
            axis=0,
        ).astype(BF)

    return rows


def outer_attn_kernel(n, depth, cols, table, x, d_qkv, d_att, ctx, attn_sums, up_sums, totals_one, totals_two, *refs):
    whole = jnp.concatenate(
        [dot(x[...], d_qkv[...], TN).astype(BF), dot(d_att[...], ctx[...], TN).astype(BF)], axis=1
    )
    units, width = up_sums.shape[1] // 2, x.shape[1]
    extra = vector_rows(
        2 * n, cols, units, width // (8 * n), table[5],
        attn_sums[...], up_sums[...], totals_one[...], totals_two[...],
    )
    for row in range(2):
        store_quarters(table, n, depth, row, by_row(whole, row, cols), refs, extra)


def outer_attn(place, table, x, d_qkv, d_att, ctx, sums, depth):
    n, cols, width = place.line_size, ctx.shape[1] // 2, x.shape[1]
    if depth % 16:
        whole = jnp.concatenate([dot(x, d_qkv, TN), dot(d_att, ctx, TN)], axis=1).astype(BF)
        extra = vector_rows(2 * n, cols, sums[1].shape[1] // 2, width // (8 * n), place.core, *sums)
        vectors = jnp.stack([extra(row, data) for row in range(2) for data in range(2 * n)])
        return spread(place, jnp.stack([by_row(whole, i, cols) for i in range(2)]), depth, vectors)
    shape = ((n, depth + EXTRA, width), BF)
    return call(
        functools.partial(outer_attn_kernel, n, depth, cols),
        [shape] * 4,
        [table, x, d_qkv, d_att, ctx] + list(sums),
        scalars=1,
    )


def head_lanes(rows, head):
    lane = lax.broadcasted_iota(jnp.int32, (rows, LANES), 1)
    return (lane < HD) if head == 0 else (lane >= HD)


def by_kind(unit, start, size):
    return jnp.concatenate([unit[0:1, start : start + size], unit[1:2, start : start + size]], axis=1)


def project_kernel(x, weights, unit, joined, qkv):
    cols = qkv.shape[1] // 3
    half = cols // 2
    for kind in range(4):
        cut = slice(kind * half, (kind + 1) * half)
        joined[:, kind * cols : (kind + 1) * cols] = jnp.concatenate(
            [weights[0, :, cut], weights[1, :, cut]], axis=1
        )
    qkv[:, :cols] = (
        (dot(x[...], joined[:, :cols]) + by_kind(unit, 0, half)).astype(BF).astype(F32) * HD ** (-0.5)
    ).astype(BF)
    qkv[:, cols : 2 * cols] = dot(x[...], joined[:, cols : 2 * cols]).astype(BF)
    qkv[:, 2 * cols :] = (dot(x[...], joined[:, 2 * cols : 3 * cols]) + by_kind(unit, half, half)).astype(BF)


def attend_kernel(block, chunk, bounds, qkv, joined, probs, ctx, part, mask):
    rows, cols = ctx.shape
    pair = pl.program_id(0)

    def labels(index):
        part_of = index // block
        place = index + jnp.where(part_of == 1, block, jnp.where(part_of == 2, -block, 0))
        total = jnp.zeros_like(index)
        for j in range(4):
            total = total + (place >= bounds[j]).astype(jnp.int32)
        return total

    @pl.when(pair == 0)
    def _():
        across = labels(lax.broadcasted_iota(jnp.int32, (1, rows), 1))
        down = labels(lax.broadcasted_iota(jnp.int32, (rows, 1), 0))
        mask[...] = jnp.where(down == across, 0.0, -1000000000.0)

    def lanes(kind):
        return pl.ds(pl.multiple_of(kind * cols + pair * LANES, LANES), LANES)

    keys, values = qkv[:, lanes(1)], qkv[:, lanes(2)]
    for step in range(rows // chunk):
        at = slice(step * chunk, (step + 1) * chunk)
        queries = qkv[at, lanes(0)]
        heads = [
            jnp.where(head_lanes(chunk, head), queries, jnp.zeros_like(queries)) for head in range(2)
        ]
        scores = [dot(one, keys, NT) + mask[at, :] for one in heads]
        exponents = [jnp.exp(one - jnp.max(one, axis=1, keepdims=True)) for one in scores]
        rates = [1.0 / jnp.sum(one, axis=1, keepdims=True) for one in exponents]
        lows = [(one * rate).astype(BF) for one, rate in zip(exponents, rates)]
        for head in range(2):
            probs[head, at, :] = lows[head]
        outs = [dot(one, values) for one in lows]
        ctx[at, lanes(0)] = jnp.where(head_lanes(chunk, 0), outs[0], outs[1]).astype(BF)

    @pl.when(pair == pl.num_programs(0) - 1)
    def _():
        part[...] = dot(ctx[...], joined[:, 3 * cols :], NT).astype(BF)


def norm_parts(values):
    centred = values - jnp.mean(values, axis=-1, keepdims=True)
    rate = lax.rsqrt(jnp.mean(centred * centred, axis=-1, keepdims=True) + 1e-06)
    return centred * rate, rate


def norm_back(grad, unit, rate, scale):
    inner = grad * scale
    return rate * (
        inner
        - jnp.mean(inner, axis=-1, keepdims=True)
        - unit * jnp.mean(inner * unit, axis=-1, keepdims=True)
    )


def start_sums(*refs):
    @pl.when(pl.program_id(0) == 0)
    def _():
        for ref in refs:
            ref[...] = jnp.zeros_like(ref)


def up_kernel(start, x, mine, other, norms, bias, weights, unit, rate, low, activated, slope):
    units = weights.shape[2]
    first_in = x[...].astype(F32) + mine[...].astype(F32) + other[...].astype(F32) + norms[2:3]
    one, scale = norm_parts(first_in)
    unit[...] = one.astype(BF)
    rate[...] = jnp.broadcast_to(scale, rate.shape)
    normed = (one * norms[0:1] + norms[3:4]).astype(BF)
    low[...] = normed
    up_bias = by_kind(bias, start, units)
    for half in range(2):
        for part in range(units // TILE):
            cut = slice(half * units + part * TILE, half * units + (part + 1) * TILE)
            value = dot(normed, weights[half, :, part * TILE : (part + 1) * TILE]) + up_bias[:, cut]
            share = 0.5 + 0.5 * lax.erf(value * (0.5**0.5))
            activated[:, cut] = (value * share).astype(BF)
            bell = jnp.exp(-0.5 * value * value) * 0.3989422804014327
            slope[:, cut] = (share + value * bell).astype(BF)


def down_kernel(depth, n, where, activated, own, first, second, far, part, whole):
    pl.when(pl.program_id(0) == 0)(
        lambda: place_kernel(depth, n, where, own, first, second, far, whole)
    )
    units = whole.shape[2]
    part[...] = (
        dot(activated[:, :units], whole[0], NT) + dot(activated[:, units:], whole[1], NT)
    ).astype(BF)


def plain_down_kernel(activated, weights, part):
    units = weights.shape[2]
    part[...] = (
        dot(activated[:, :units], weights[0], NT) + dot(activated[:, units:], weights[1], NT)
    ).astype(BF)


def down(place, activated, quarters, depth):
    n, _, units = quarters[0].shape
    rows, width = activated.shape[0], 2 * n * depth
    if depth % 16:
        weights = place_group(place, quarters, depth)[0]
        part = call(
            plain_down_kernel, [((rows, width), BF, True)], [(activated, True), weights], steps=2
        )[0]
        return part, weights
    return call(
        functools.partial(down_kernel, depth, n),
        [((rows, width), BF, True), ((2, width, units), BF)],
        [place_spots(place), (activated, True)] + list(quarters),
        scalars=1,
        steps=2,
    )


def column_sums(totals, index, value):
    totals[index : index + 1, :] = totals[index : index + 1, :] + jnp.sum(value, axis=0, keepdims=True)


def second_kernel(unit, mine, other, grad, norms, result, d_mixed, totals):
    start_sums(totals)
    normed = unit[...].astype(F32) * norms[0:1] + norms[3:4]
    one, rate = norm_parts(normed + mine[...].astype(F32) + other[...].astype(F32) + norms[4:5])
    result[...] = (one * norms[1:2] + norms[5:6]).astype(BF)
    dy = grad[...].astype(F32)
    back = norm_back(dy, one, rate, norms[1:2])
    d_mixed[...] = back.astype(BF)
    column_sums(totals, 0, dy * one)
    column_sums(totals, 1, back)
    column_sums(totals, 2, dy)


def hidden_back_kernel(d_mixed, down, up, slope, d_hidden, part, sums):
    units = down.shape[2]
    start_sums(sums)
    total = 0.0
    for half in range(2):
        cut = slice(half * units, (half + 1) * units)
        low = (dot(d_mixed[...], down[half]) * slope[:, cut].astype(F32)).astype(BF)
        d_hidden[:, cut] = low
        sums[0:1, cut] = sums[0:1, cut] + jnp.sum(low.astype(F32), axis=0, keepdims=True)
        total += dot(low, up[half], NT)
    part[...] = total.astype(BF)


def first_back_kernel(d_second, mine, other, unit, rate, norms, joined, d_att, d_ctx, totals):
    cols = d_ctx.shape[1]
    start_sums(totals)
    d_first = d_second[...].astype(F32) + mine[...].astype(F32) + other[...].astype(F32)
    one = unit[...].astype(F32)
    back = norm_back(d_first, one, rate[:, 0:1], norms[0:1])
    low = back.astype(BF)
    d_att[...] = low
    column_sums(totals, 0, d_first * one)
    column_sums(totals, 1, back)
    column_sums(totals, 2, d_first)
    d_ctx[...] = dot(low, joined[:, 3 * cols :]).astype(BF)


def attend_back_kernel(chunk, d_ctx, qkv, probs, ctx, d_qkv, sums, d_scores):
    rows, cols = ctx.shape
    pair = pl.program_id(0)
    start_sums(sums)

    def lanes(kind):
        return pl.ds(pl.multiple_of(kind * cols + pair * LANES, LANES), LANES)

    keys, values = qkv[:, lanes(1)], qkv[:, lanes(2)]
    for step in range(rows // chunk):
        at = slice(step * chunk, (step + 1) * chunk)
        grads = d_ctx[at, lanes(0)]
        with_context = grads.astype(F32) * ctx[at, lanes(0)].astype(F32)
        inside = [head_lanes(chunk, head) for head in range(2)]
        ones = [jnp.where(lane, grads, jnp.zeros_like(grads)) for lane in inside]
        d_probs = [dot(one, values, NT) for one in ones]
        inner = [jnp.sum(jnp.where(lane, with_context, 0.0), axis=1, keepdims=True) for lane in inside]
        lows = [
            (probs[head, at, :].astype(F32) * (d_probs[head] - inner[head])).astype(BF)
            for head in range(2)
        ]
        for head in range(2):
            d_scores[head, at, :] = lows[head]
        outs = [dot(one, keys) for one in lows]
        d_queries = (jnp.where(head_lanes(chunk, 0), outs[0], outs[1]) * HD ** (-0.5)).astype(BF)
        d_qkv[at, lanes(0)] = d_queries
        sums[0:1, lanes(0)] = sums[0:1, lanes(0)] + jnp.sum(
            d_queries.astype(F32), axis=0, keepdims=True
        )
    d_keys, d_values = 0.0, 0.0
    for head in range(2):
        inside = head_lanes(rows, head)
        queries, grads = qkv[:, lanes(0)], d_ctx[:, lanes(0)]
        d_keys += dot(d_scores[head], jnp.where(inside, queries, jnp.zeros_like(queries)), TN)
        d_values += dot(probs[head], jnp.where(inside, grads, jnp.zeros_like(grads)), TN)
    d_qkv[:, lanes(1)] = d_keys.astype(BF)
    d_values = d_values.astype(BF)
    d_qkv[:, lanes(2)] = d_values
    sums[0:1, lanes(1)] = jnp.sum(d_values.astype(F32), axis=0, keepdims=True)


def inputs_kernel(d_qkv, joined, part):
    part[...] = dot(d_qkv[...], joined[:, : d_qkv.shape[1]], NT).astype(BF)


def pack_kernel(w_qkv, w_out_t, unit_bias, norm_gain, norm_bias, attn):
    depth, cols, width = w_qkv.shape[1], w_qkv.shape[2], attn.shape[1]
    for kind in range(3):
        attn[:depth, kind * cols : (kind + 1) * cols] = w_qkv[kind]
    attn[:depth, 3 * cols :] = w_out_t[...]
    small = [ref[...].astype(F32) for ref in (unit_bias, norm_gain, norm_bias)]
    small = [jnp.pad(value, ((0, 0), (0, width - value.shape[1]))) for value in small]
    small.append(jnp.zeros((EXTRA - 7, width), F32))
    attn[depth:, :] = jnp.concatenate(small, axis=0).astype(BF)


def unpack_kernel(count, own, *refs):
    parts, (qkv, out, unit, gain, bias) = refs[:count], refs[count:]
    total = own[...]
    for part in parts:
        total = total + part[...].astype(F32)
    depth, cols = qkv.shape[1], qkv.shape[2]
    for kind in range(3):
        qkv[kind] = total[:depth, kind * cols : (kind + 1) * cols]
    out[...] = total[:depth, 3 * cols :].T
    extra = total[depth:]
    unit[...] = extra[0:1, : unit.shape[1]]
    gain[...] = extra[1:3, : gain.shape[1]]
    bias[...] = extra[3:7, : bias.shape[1]]


def unpack(own, parts, depth, cols, share, small):
    outs = [
        ((3, depth, cols), F32),
        ((cols, depth), F32),
        ((1, share), F32),
        ((2, small), F32),
        ((4, small), F32),
    ]
    if depth % 16 == 0:
        return call(functools.partial(unpack_kernel, len(parts)), outs, [own] + list(parts))
    total = total_of(own, parts)
    return (
        jnp.stack([total[:depth, t * cols : (t + 1) * cols] for t in range(3)]),
        total[:depth, 3 * cols :].T,
        total[depth : depth + 1, :share],
        total[depth + 1 : depth + 3, :small],
        total[depth + 3 : depth + 7, :small],
    )


def body(
    inputs, w_qkv, w_out, w_up, w_down, unit_bias, norm_gain, norm_bias, seq_lengths, cotangent
):
    place = Place()
    row, core = place.row, place.core
    groups = place.groups
    block, width = inputs.shape[1], inputs.shape[2]
    rows = 4 * block
    depth, head_cols = w_qkv.shape[1], w_qkv.shape[2]
    units = w_up.shape[1]
    share = unit_bias.shape[1]
    small = norm_gain.shape[1]
    cols = 2 * head_cols
    heads = cols // HD

    if depth % 16 == 0:
        (attn_shard,) = call(
            pack_kernel,
            [((depth + EXTRA, width), BF)],
            [w_qkv, w_out.T, unit_bias, norm_gain, norm_bias],
        )
    else:
        small_rows = [
            jnp.pad(part, ((0, 0), (0, width - part.shape[1]))) for part in (unit_bias, norm_gain, norm_bias)
        ]
        small_rows.append(jnp.zeros((EXTRA - 7, width), BF))
        attn_shard = jnp.concatenate([w_qkv[0], w_qkv[1], w_qkv[2], w_out.T], axis=1)
        attn_shard = jnp.concatenate([attn_shard] + small_rows, axis=0)
    keep = lambda array, index: lax.dynamic_index_in_dim(array, index, 0, keepdims=False)
    outgoing = jnp.stack([keep(inputs, 1 - row), keep(cotangent, 1 - row)])
    incoming = place.row_swap(outgoing)
    attn_own = jnp.stack(line_parts(place, after(attn_shard, outgoing)))
    attn_own = after(attn_own, incoming)
    attn_first, attn_second = place.cross(attn_own, 0), place.cross(attn_own, 1)
    up_own = jnp.stack(line_parts(place, after(w_up, attn_own)))
    attn_first = after(attn_first, attn_second, up_own)
    attn_far = place.cross(attn_first, 1)
    up_own = after(up_own, attn_first)
    up_first, up_second = place.cross(up_own, 0), place.cross(up_own, 1)
    down_own = jnp.stack(line_parts(place, after(w_down.T, up_own)))

    mine = jnp.stack([keep(inputs, row), keep(cotangent, row)])
    low_rows = jnp.where(row == 0, mine, incoming)
    high_rows = jnp.where(row == 0, incoming, mine)
    half = jnp.concatenate([low_rows, high_rows], axis=1)
    other = place.core_swap(half)
    both = jnp.where(
        core == 0,
        jnp.concatenate([half, other], axis=1),
        jnp.concatenate([other, half], axis=1),
    )
    x, grad_rows = both[0], both[1]

    attn_whole, extras, unit_bias = place_group(
        place, (attn_own, attn_first, attn_second, attn_far), depth, share
    )
    norm_here = extras[:, :, 1:7, :small]
    norm_there = place.core_swap(norm_here)
    norm_all = jnp.where(
        core == 0,
        jnp.stack([norm_here, norm_there], axis=2),
        jnp.stack([norm_there, norm_here], axis=2),
    )
    norm_all = jnp.transpose(norm_all, (3, 1, 0, 2, 4)).reshape(6, width).astype(F32)
    norms = jnp.pad(norm_all, ((0, 2), (0, 0)))
    table = place.roles()

    bounds = jnp.cumsum(keep(seq_lengths, row), dtype=jnp.int32)
    wide = rows * width
    joined, qkv = call(
        project_kernel,
        [((width, 4 * cols), BF), ((rows, 3 * cols), BF)],
        [x, attn_whole, unit_bias],
    )
    up_first = after(up_first, up_second, down_own, qkv)
    up_far = place.cross(up_first, 1)
    down_own = after(down_own, up_first)
    down_first, down_second = place.cross(down_own, 0), place.cross(down_own, 1)
    probs, ctx, part = call(
        functools.partial(attend_kernel, block, rows),
        [((heads, rows, rows), BF, True), ((rows, cols), BF), ((rows, width), BF)],
        [bounds, after(qkv, up_first, norms), joined],
        scalars=1,
        scratch=[pltpu.VMEM((rows, rows), F32)],
        steps=cols // LANES,
    )
    down_first = after(down_first, down_second, ctx)
    down_far = place.cross(down_first, 1)
    up_far = after(up_far, down_first)
    up_whole = place_group(place, (up_own, up_first, up_second, up_far), depth)[0]
    unit, rate, first_low, activated, slope = call(
        functools.partial(up_kernel, 2 * head_cols),
        [
            ((rows, width), BF, True),
            ((rows, LANES), F32, True),
            ((rows, width), BF, True),
            ((rows, 2 * units), BF, True),
            ((rows, 2 * units), BF, True),
        ],
        [(x, True), (part, True), (place.core_swap(part), True), norms, unit_bias, up_whole],
        steps=2,
    )
    part, down_whole = down(place, activated, (down_own, down_first, down_second, down_far), depth)
    result, d_mixed, totals_two = call(
        second_kernel,
        [((rows, width), BF, True), ((rows, width), BF, True), ((8, width), F32)],
        [(unit, True), (part, True), (place.core_swap(part), True), (grad_rows, True), norms],
        steps=2,
    )

    down_own, down_first, down_second, down_far = outer(place, table, d_mixed, activated, depth)
    down_got_far = place.cross(down_far, 0)
    d_hidden, part, up_sums = call(
        hidden_back_kernel,
        [((rows, 2 * units), BF, True), ((rows, width), BF, True), ((8, 2 * units), F32)],
        [(after(d_mixed, down_far), True), down_whole, up_whole, (slope, True)],
        steps=2,
    )
    add = lambda one, other: (one.astype(F32) + other.astype(F32)).astype(BF)
    add_three = lambda one, two, three: one.astype(F32) + two.astype(F32) + three.astype(F32)
    up_own, up_first, up_second, up_far = outer(place, table, first_low, d_hidden, depth)
    down_second = add(down_second, after(down_got_far, up_far))
    down_got_second = place.cross(down_second, 1)
    down_got_first = place.cross(after(down_first, down_far), 0)
    up_got_far = place.cross(after(up_far, down_second), 0)
    d_att, d_ctx, totals_one = call(
        first_back_kernel,
        [((rows, width), BF, True), ((rows, cols), BF, True), ((8, width), F32)],
        [
            (after(d_mixed, down_second), True),
            (part, True),
            (place.core_swap(part), True),
            (unit, True),
            (rate, True),
            norms,
            joined,
        ],
        steps=2,
    )
    d_qkv, attn_sums = call(
        functools.partial(attend_back_kernel, rows),
        [((rows, 3 * cols), BF), ((8, 2 * cols), F32)],
        [d_ctx, qkv, (probs, True), ctx],
        scratch=[pltpu.VMEM((2, rows, rows), BF)],
        steps=cols // LANES,
    )
    attn_own, attn_first, attn_second, attn_far = outer_attn(
        place, table, x, d_qkv, d_att, ctx,
        (attn_sums, up_sums, totals_one, totals_two), depth,
    )
    attn_got_far = place.cross(attn_far, 0)
    up_second = add(up_second, after(up_got_far, attn_far))
    up_got_second = place.cross(up_second, 1)
    up_got_first = place.cross(after(up_first, up_second), 0)
    down_sum = add_three(down_own, down_got_first, after(down_got_second, up_second))
    down_parts = scatter_parts(place, down_sum)
    (part,) = call(
        inputs_kernel,
        [((rows, width), BF, True)],
        [(after(d_qkv, down_sum), True), joined],
        steps=2,
    )
    grad_in = d_att.astype(F32) + part.astype(F32) + place.core_swap(part).astype(F32)
    attn_second = add(attn_second, after(attn_got_far, part))
    attn_got_second = place.cross(attn_second, 1)
    attn_got_first = place.cross(after(attn_first, attn_second), 0)
    grad_down = total_of(down_sum[0], down_parts)
    up_sum = add_three(up_own, up_got_first, after(up_got_second, attn_second))
    up_parts = scatter_parts(place, up_sum)
    attn_sum = add_three(attn_own, after(attn_got_first, *down_parts, *up_parts), attn_got_second)
    attn_start, attn_parts = attn_sum[0], scatter_parts(place, attn_sum)
    grad_up = total_of(up_sum[0], up_parts)

    def hand_back(full):
        mine = lax.dynamic_slice_in_dim(full, core * 2 * block, 2 * block, 0)
        mine = mine.reshape(2, block, width)
        kept = keep(mine, row)
        got = place.row_swap(after(keep(mine, 1 - row).astype(BF), attn_sum)).astype(full.dtype)
        return jnp.where(row == 0, jnp.stack([kept, got]), jnp.stack([got, kept]))

    outputs, grad_inputs = hand_back(result), hand_back(grad_in)
    attn_parts = [after(part, outputs, grad_inputs) for part in attn_parts]
    grad_qkv, grad_out, grad_unit, grad_gain, grad_bias = unpack(
        attn_start, attn_parts, depth, head_cols, share, small
    )
    return (
        outputs,
        grad_inputs,
        grad_qkv,
        grad_out,
        grad_up,
        jnp.transpose(grad_down),
        grad_unit,
        grad_gain,
        grad_bias,
    )


def solution(mesh):
    placed = (
        P("dp", "mp", None),
        P(None, "dp", "mp"),
        P("mp", "dp"),
        P("dp", "mp"),
        P("mp", "dp"),
        P("mp", "dp"),
        P(None, ("dp", "mp")),
        P(None, ("dp", "mp")),
        P("dp", None),
        P("dp", "mp", None),
    )
    return jax.shard_map(
        body,
        mesh=mesh,
        in_specs=placed,
        out_specs=(
            P("dp", "mp", None),
            P("dp", "mp", None),
            P(None, "dp", "mp"),
            P("mp", "dp"),
            P("dp", "mp"),
            P("mp", "dp"),
            P("mp", "dp"),
            P(None, ("dp", "mp")),
            P(None, ("dp", "mp")),
        ),
        check_vma=False,
    )
```

```python
import functools

import jax
import jax.numpy as jnp
from jax import lax
from jax.experimental import pallas as pl
from jax.experimental.pallas import tpu as pltpu
from jax.sharding import PartitionSpec as P

HD = 64
LANES = 128
TILE = 256
EXTRA = 16
BF = jnp.bfloat16
F32 = jnp.float32
LIMIT = 28 * 1024 * 1024
NN = ((1,), (0,))
NT = ((1,), (1,))
TN = ((0,), (0,))


def dot(left, right, dims=NN):
    return lax.dot_general(left, right, (dims, ((), ())), preferred_element_type=F32)


def call(kernel, outs, args, scalars=0, scratch=(), steps=None):
    args = [arg if isinstance(arg, tuple) else (arg, False) for arg in args]
    outs = [out if len(out) == 3 else out + (False,) for out in outs]

    def spec(shape, cut):
        if steps is None:
            return pl.BlockSpec(memory_space=pltpu.VMEM)
        if cut:
            rest = (0,) * (len(shape) - 1)
            return pl.BlockSpec((shape[0] // steps,) + tuple(shape[1:]), lambda i: (i,) + rest)
        return pl.BlockSpec(tuple(shape), lambda i: (0,) * len(shape))

    return pl.pallas_call(
        kernel,
        out_shape=[jax.ShapeDtypeStruct(shape, kind) for shape, kind, _ in outs],
        grid=() if steps is None else (steps,),
        in_specs=[pl.BlockSpec(memory_space=pltpu.SMEM)] * scalars
        + [spec(arg.shape, cut) for arg, cut in args[scalars:]],
        out_specs=[spec(shape, cut) for shape, _, cut in outs],
        scratch_shapes=list(scratch),
        compiler_params=pltpu.CompilerParams(vmem_limit_bytes=LIMIT),
        cost_estimate=pl.CostEstimate(flops=8000000000, bytes_accessed=10000000, transcendentals=0),
    )(*[arg for arg, _ in args])


def after(value, *others):
    return lax.optimization_barrier((value,) + others)[0]


class Place:
    def __init__(self):
        self.groups = lax.axis_size("dp")
        self.line_size = self.groups // 2
        data, model = lax.axis_index("dp"), lax.axis_index("mp")
        self.line, self.pair = data // 2, data % 2
        self.row, self.core = model // 2, model % 2

    def core_swap(self, value):
        return lax.ppermute(value, "mp", [(0, 1), (1, 0), (2, 3), (3, 2)])

    def row_swap(self, value):
        return lax.ppermute(value, "mp", [(0, 2), (2, 0), (1, 3), (3, 1)])

    def line_swap(self, value, step):
        pairs = [(i, i ^ (2 * step)) for i in range(self.groups)]
        return lax.ppermute(value, "dp", pairs)

    def cross(self, value, along_row):
        pairs = []
        for data in range(self.groups):
            for model in range(4):
                if model % 2 == along_row:
                    pairs.append((data * 4 + model, data * 4 + (model ^ 2)))
                else:
                    pairs.append((data * 4 + model, (data ^ 1) * 4 + model))
        return lax.ppermute(value, ("dp", "mp"), pairs)

    def quarters(self):
        other_row, other_pair = 1 - self.row, 1 - self.pair
        swap = self.core == 0
        first = (jnp.where(swap, other_row, self.row), jnp.where(swap, self.pair, other_pair))
        second = (jnp.where(swap, self.row, other_row), jnp.where(swap, other_pair, self.pair))
        return (self.row, self.pair), first, second, (other_row, other_pair)

    def roles(self):
        found = []
        for row in range(2):
            for pair in range(2):
                other_row, other_pair = self.row != row, self.pair != pair
                near, far = (other_row, other_pair)
                near = jnp.where(self.core == 0, other_row, other_pair)
                far = jnp.where(self.core == 0, other_pair, other_row)
                found.append(near.astype(jnp.int32) + 2 * far.astype(jnp.int32))
        return jnp.stack(found + [self.line, self.core]).astype(jnp.int32)


def line_parts(place, shard):
    n = place.line_size
    if n <= 4:
        return [shard] + [place.line_swap(shard, step) for step in range(1, n)]
    held, step = shard[None], 1
    while step < n:
        held, step = jnp.concatenate([held, place.line_swap(held, step)]), step * 2
    return [held[i] for i in range(n)]


def scatter_parts(place, terms):
    n = place.line_size
    if n <= 4:
        low = terms.astype(BF)
        return [place.line_swap(low[step], step) for step in range(1, n)]
    first, step = terms[0], n // 2
    while step:
        got = place.line_swap(terms[step:].astype(BF), step)
        terms, step = terms[:step] + got.astype(F32), step // 2
    return [terms[0] - first]


def total_of(start, parts):
    for part in parts:
        start = start + part.astype(F32)
    return start


def place_kernel(depth, n, where, own, first, second, far, whole, extras=None):
    for quarter, source in enumerate((own, first, second, far)):
        row, pair = where[2 * quarter], where[2 * quarter + 1]
        for step in range(n):
            data = jnp.bitwise_xor(where[8], step) * 2 + pair
            start = pl.multiple_of(data * depth, 16)
            whole[row, pl.ds(start, depth), :] = source[step, :depth]
            if extras is not None:
                extras[row, data] = source[step, depth:]


def place_attn_kernel(depth, n, share, where, own, first, second, far, whole, extras, unit):
    place_kernel(depth, n, where, own, first, second, far, whole, extras)
    unit[...] = jnp.zeros_like(unit)
    for row in range(2):
        for data in range(2 * n):
            value = extras[row, data].astype(F32)
            unit[row : row + 1, data * share : (data + 1) * share] = value[0:1, :share]


def place_spots(place):
    spots = [scalar for spot in place.quarters() for scalar in spot] + [place.line]
    return jnp.stack(spots).astype(jnp.int32)


def place_group(place, quarters, depth, share=None):
    n, rows, width = quarters[0].shape
    kind = quarters[0].dtype
    outs = [((2, 2 * n * depth, width), kind)]
    if share is not None:
        outs += [((2, 2 * n, EXTRA, width), kind), ((8, 2 * n * share), F32)]
    if depth % 16 == 0:
        kernel = functools.partial(place_kernel, depth, n)
        if share is not None:
            kernel = functools.partial(place_attn_kernel, depth, n, share)
        return call(kernel, outs, [place_spots(place)] + list(quarters), scalars=1)
    whole = jnp.zeros((2, n, 2, rows, width), kind)
    for piece, (row, pair) in zip(quarters, place.quarters()):
        for step in range(n):
            start = (row, place.line ^ step, pair, 0, 0)
            whole = lax.dynamic_update_slice(whole, piece[step][None, None, None], start)
    out = [whole[:, :, :, :depth].reshape(outs[0][0])]
    if share is not None:
        extras = whole[:, :, :, depth:].reshape(outs[1][0])
        unit = extras[:, :, 0, :share].reshape(2, 2 * n * share).astype(F32)
        out += [extras, jnp.pad(unit, ((0, 6), (0, 0)))]
    return out


def spread(place, terms, depth, vectors=None):
    n = place.line_size
    terms = terms.reshape(2, n, 2, depth, terms.shape[-1])
    if vectors is not None:
        vectors = jnp.pad(vectors, ((0, 0), (0, 0), (0, terms.shape[-1] - vectors.shape[-1])))
        vectors = vectors.reshape(2, n, 2, EXTRA, -1)
        terms = jnp.concatenate([terms, vectors.astype(terms.dtype)], axis=3)
    order = lax.iota(jnp.int32, n) ^ place.line
    terms = jnp.take(terms, order, axis=1)

    def quarter(at):
        size = (1, n, 1) + terms.shape[3:]
        return lax.dynamic_slice(terms, (at[0], 0, at[1], 0, 0), size).reshape((n,) + terms.shape[3:])

    return [quarter(at) for at in place.quarters()]


def store_quarters(table, n, depth, row, value, refs, extra=None):
    for pair in range(2):
        role = table[row * 2 + pair]

        def put(ref):
            for line in range(n):
                at = jnp.bitwise_xor(table[4], line)
                data = line * 2 + pair
                ref[at, :depth] = value[data * depth : (data + 1) * depth]
                if extra is not None:
                    rows = extra(row, data)
                    known = rows.shape[1]
                    ref[at, depth:, :known] = rows
                    ref[at, depth:, known:] = jnp.zeros((EXTRA, ref.shape[2] - known), BF)

        for index in range(4):
            pl.when(role == index)(functools.partial(put, refs[index]))


def outer_kernel(n, depth, table, left, right, *refs):
    width = refs[0].shape[-1]
    turned = left[...].T
    for row in range(2):
        value = dot(turned, right[:, row * width : (row + 1) * width]).astype(BF)
        store_quarters(table, n, depth, row, value, refs)


def outer(place, table, left, right, depth):
    n, width = place.line_size, right.shape[1] // 2
    if depth % 16:
        halves = [dot(left, right[:, i * width : (i + 1) * width], TN).astype(BF) for i in range(2)]
        return spread(place, jnp.stack(halves), depth)
    shape = ((n, depth, width), BF)
    return call(
        functools.partial(outer_kernel, n, depth),
        [shape] * 4,
        [table, left, right],
        scalars=1,
    )


def by_row(value, row, cols):
    kinds = value.shape[1] // (2 * cols)
    return jnp.concatenate(
        [value[:, (2 * t + row) * cols : (2 * t + row + 1) * cols] for t in range(kinds)], axis=1
    )


def vector_rows(groups, cols, units, small, core, attn_sums, up_sums, totals_one, totals_two):
    share = (2 * cols + units) // groups
    known = -(-share // LANES) * LANES
    norms = jnp.concatenate(
        [totals_one[0:1], totals_two[0:1], totals_one[1:3], totals_two[1:3]], axis=0
    )

    def line(row):
        at = slice(row * cols, (row + 1) * cols)
        later = slice((2 + row) * cols, (3 + row) * cols)
        return jnp.concatenate(
            [attn_sums[0:1, at], attn_sums[0:1, later], up_sums[0:1, row * units : (row + 1) * units]], axis=1
        )

    lines = [line(row) for row in range(2)]

    def rows(row, data):
        first = lines[row][:, data * share : (data + 1) * share]
        start = (data * 4 + row * 2) * small
        norm = jnp.where(core == 0, norms[:, start : start + small], norms[:, start + small : start + 2 * small])
        return jnp.concatenate(
            [
                jnp.pad(first, ((0, 0), (0, known - share))),
                jnp.pad(norm, ((0, 0), (0, known - small))),
                jnp.zeros((EXTRA - 7, known), F32),
            ],
            axis=0,
        ).astype(BF)

    return rows


def outer_attn_kernel(n, depth, cols, table, x, d_qkv, d_att, ctx, attn_sums, up_sums, totals_one, totals_two, *refs):
    whole = jnp.concatenate(
        [dot(x[...], d_qkv[...], TN).astype(BF), dot(d_att[...], ctx[...], TN).astype(BF)], axis=1
    )
    units, width = up_sums.shape[1] // 2, x.shape[1]
    extra = vector_rows(
        2 * n, cols, units, width // (8 * n), table[5],
        attn_sums[...], up_sums[...], totals_one[...], totals_two[...],
    )
    for row in range(2):
        store_quarters(table, n, depth, row, by_row(whole, row, cols), refs, extra)


def outer_attn(place, table, x, d_qkv, d_att, ctx, sums, depth):
    n, cols, width = place.line_size, ctx.shape[1] // 2, x.shape[1]
    if depth % 16:
        whole = jnp.concatenate([dot(x, d_qkv, TN), dot(d_att, ctx, TN)], axis=1).astype(BF)
        extra = vector_rows(2 * n, cols, sums[1].shape[1] // 2, width // (8 * n), place.core, *sums)
        vectors = jnp.stack([extra(row, data) for row in range(2) for data in range(2 * n)])
        return spread(place, jnp.stack([by_row(whole, i, cols) for i in range(2)]), depth, vectors)
    shape = ((n, depth + EXTRA, width), BF)
    return call(
        functools.partial(outer_attn_kernel, n, depth, cols),
        [shape] * 4,
        [table, x, d_qkv, d_att, ctx] + list(sums),
        scalars=1,
    )


def head_lanes(rows, head):
    lane = lax.broadcasted_iota(jnp.int32, (rows, LANES), 1)
    return (lane < HD) if head == 0 else (lane >= HD)


def by_kind(unit, start, size):
    return jnp.concatenate([unit[0:1, start : start + size], unit[1:2, start : start + size]], axis=1)


def project_kernel(x, weights, unit, joined, qkv):
    cols = qkv.shape[1] // 3
    half = cols // 2
    for kind in range(4):
        cut = slice(kind * half, (kind + 1) * half)
        joined[:, kind * cols : (kind + 1) * cols] = jnp.concatenate(
            [weights[0, :, cut], weights[1, :, cut]], axis=1
        )
    qkv[:, :cols] = (
        (dot(x[...], joined[:, :cols]) + by_kind(unit, 0, half)).astype(BF).astype(F32) * HD ** (-0.5)
    ).astype(BF)
    qkv[:, cols : 2 * cols] = dot(x[...], joined[:, cols : 2 * cols]).astype(BF)
    qkv[:, 2 * cols :] = (dot(x[...], joined[:, 2 * cols : 3 * cols]) + by_kind(unit, half, half)).astype(BF)


def attend_kernel(block, chunk, bounds, qkv, joined, probs, ctx, part, mask):
    rows, cols = ctx.shape
    pair = pl.program_id(0)

    def labels(index):
        part_of = index // block
        place = index + jnp.where(part_of == 1, block, jnp.where(part_of == 2, -block, 0))
        total = jnp.zeros_like(index)
        for j in range(4):
            total = total + (place >= bounds[j]).astype(jnp.int32)
        return total

    @pl.when(pair == 0)
    def _():
        across = labels(lax.broadcasted_iota(jnp.int32, (1, rows), 1))
        down = labels(lax.broadcasted_iota(jnp.int32, (rows, 1), 0))
        mask[...] = jnp.where(down == across, 0.0, -1000000000.0)

    def lanes(kind):
        return pl.ds(pl.multiple_of(kind * cols + pair * LANES, LANES), LANES)

    keys, values = qkv[:, lanes(1)], qkv[:, lanes(2)]
    for step in range(rows // chunk):
        at = slice(step * chunk, (step + 1) * chunk)
        queries = qkv[at, lanes(0)]
        heads = [
            jnp.where(head_lanes(chunk, head), queries, jnp.zeros_like(queries)) for head in range(2)
        ]
        scores = [dot(one, keys, NT) + mask[at, :] for one in heads]
        exponents = [jnp.exp(one - jnp.max(one, axis=1, keepdims=True)) for one in scores]
        rates = [1.0 / jnp.sum(one, axis=1, keepdims=True) for one in exponents]
        lows = [(one * rate).astype(BF) for one, rate in zip(exponents, rates)]
        for head in range(2):
            probs[head, at, :] = lows[head]
        outs = [dot(one, values) for one in lows]
        ctx[at, lanes(0)] = jnp.where(head_lanes(chunk, 0), outs[0], outs[1]).astype(BF)

    @pl.when(pair == pl.num_programs(0) - 1)
    def _():
        part[...] = dot(ctx[...], joined[:, 3 * cols :], NT).astype(BF)


def norm_parts(values):
    centred = values - jnp.mean(values, axis=-1, keepdims=True)
    rate = lax.rsqrt(jnp.mean(centred * centred, axis=-1, keepdims=True) + 1e-06)
    return centred * rate, rate


def norm_back(grad, unit, rate, scale):
    inner = grad * scale
    return rate * (
        inner
        - jnp.mean(inner, axis=-1, keepdims=True)
        - unit * jnp.mean(inner * unit, axis=-1, keepdims=True)
    )


def start_sums(*refs):
    @pl.when(pl.program_id(0) == 0)
    def _():
        for ref in refs:
            ref[...] = jnp.zeros_like(ref)


def up_kernel(start, x, mine, other, norms, bias, weights, unit, rate, low, activated, slope):
    units = weights.shape[2]
    first_in = x[...].astype(F32) + mine[...].astype(F32) + other[...].astype(F32) + norms[2:3]
    one, scale = norm_parts(first_in)
    unit[...] = one.astype(BF)
    rate[...] = jnp.broadcast_to(scale, rate.shape)
    normed = (one * norms[0:1] + norms[3:4]).astype(BF)
    low[...] = normed
    up_bias = by_kind(bias, start, units)
    for half in range(2):
        for part in range(units // TILE):
            cut = slice(half * units + part * TILE, half * units + (part + 1) * TILE)
            value = dot(normed, weights[half, :, part * TILE : (part + 1) * TILE]) + up_bias[:, cut]
            share = 0.5 + 0.5 * lax.erf(value * (0.5**0.5))
            activated[:, cut] = (value * share).astype(BF)
            bell = jnp.exp(-0.5 * value * value) * 0.3989422804014327
            slope[:, cut] = (share + value * bell).astype(BF)


def down_kernel(depth, n, where, activated, own, first, second, far, part, whole):
    pl.when(pl.program_id(0) == 0)(
        lambda: place_kernel(depth, n, where, own, first, second, far, whole)
    )
    units = whole.shape[2]
    part[...] = (
        dot(activated[:, :units], whole[0], NT) + dot(activated[:, units:], whole[1], NT)
    ).astype(BF)


def plain_down_kernel(activated, weights, part):
    units = weights.shape[2]
    part[...] = (
        dot(activated[:, :units], weights[0], NT) + dot(activated[:, units:], weights[1], NT)
    ).astype(BF)


def down(place, activated, quarters, depth):
    n, _, units = quarters[0].shape
    rows, width = activated.shape[0], 2 * n * depth
    if depth % 16:
        weights = place_group(place, quarters, depth)[0]
        part = call(
            plain_down_kernel, [((rows, width), BF, True)], [(activated, True), weights], steps=2
        )[0]
        return part, weights
    return call(
        functools.partial(down_kernel, depth, n),
        [((rows, width), BF, True), ((2, width, units), BF)],
        [place_spots(place), (activated, True)] + list(quarters),
        scalars=1,
        steps=2,
    )


def column_sums(totals, index, value):
    totals[index : index + 1, :] = totals[index : index + 1, :] + jnp.sum(value, axis=0, keepdims=True)


def second_kernel(low, mine, other, grad, norms, result, d_mixed, totals):
    start_sums(totals)
    one, rate = norm_parts(low[...].astype(F32) + mine[...].astype(F32) + other[...].astype(F32) + norms[4:5])
    result[...] = (one * norms[1:2] + norms[5:6]).astype(BF)
    dy = grad[...].astype(F32)
    back = norm_back(dy, one, rate, norms[1:2])
    d_mixed[...] = back.astype(BF)
    column_sums(totals, 0, dy * one)
    column_sums(totals, 1, back)
    column_sums(totals, 2, dy)


def hidden_back_kernel(d_mixed, down, up, slope, d_hidden, part, sums):
    units = down.shape[2]
    start_sums(sums)
    total = 0.0
    for half in range(2):
        cut = slice(half * units, (half + 1) * units)
        low = (dot(d_mixed[...], down[half]) * slope[:, cut].astype(F32)).astype(BF)
        d_hidden[:, cut] = low
        sums[0:1, cut] = sums[0:1, cut] + jnp.sum(low.astype(F32), axis=0, keepdims=True)
        total += dot(low, up[half], NT)
    part[...] = total.astype(BF)


def first_back_kernel(d_second, mine, other, unit, rate, norms, joined, d_att, d_ctx, totals):
    cols = d_ctx.shape[1]
    start_sums(totals)
    d_first = d_second[...].astype(F32) + mine[...].astype(F32) + other[...].astype(F32)
    one = unit[...].astype(F32)
    back = norm_back(d_first, one, rate[:, 0:1], norms[0:1])
    low = back.astype(BF)
    d_att[...] = low
    column_sums(totals, 0, d_first * one)
    column_sums(totals, 1, back)
    column_sums(totals, 2, d_first)
    d_ctx[...] = dot(low, joined[:, 3 * cols :]).astype(BF)


def attend_back_kernel(chunk, d_ctx, qkv, probs, ctx, d_qkv, sums, d_scores):
    rows, cols = ctx.shape
    pair = pl.program_id(0)
    start_sums(sums)

    def lanes(kind):
        return pl.ds(pl.multiple_of(kind * cols + pair * LANES, LANES), LANES)

    keys, values = qkv[:, lanes(1)], qkv[:, lanes(2)]
    for step in range(rows // chunk):
        at = slice(step * chunk, (step + 1) * chunk)
        grads = d_ctx[at, lanes(0)]
        with_context = grads.astype(F32) * ctx[at, lanes(0)].astype(F32)
        inside = [head_lanes(chunk, head) for head in range(2)]
        ones = [jnp.where(lane, grads, jnp.zeros_like(grads)) for lane in inside]
        d_probs = [dot(one, values, NT) for one in ones]
        inner = [jnp.sum(jnp.where(lane, with_context, 0.0), axis=1, keepdims=True) for lane in inside]
        lows = [
            (probs[head, at, :].astype(F32) * (d_probs[head] - inner[head])).astype(BF)
            for head in range(2)
        ]
        for head in range(2):
            d_scores[head, at, :] = lows[head]
        outs = [dot(one, keys) for one in lows]
        d_queries = (jnp.where(head_lanes(chunk, 0), outs[0], outs[1]) * HD ** (-0.5)).astype(BF)
        d_qkv[at, lanes(0)] = d_queries
        sums[0:1, lanes(0)] = sums[0:1, lanes(0)] + jnp.sum(
            d_queries.astype(F32), axis=0, keepdims=True
        )
    d_keys, d_values = 0.0, 0.0
    for head in range(2):
        inside = head_lanes(rows, head)
        queries, grads = qkv[:, lanes(0)], d_ctx[:, lanes(0)]
        d_keys += dot(d_scores[head], jnp.where(inside, queries, jnp.zeros_like(queries)), TN)
        d_values += dot(probs[head], jnp.where(inside, grads, jnp.zeros_like(grads)), TN)
    d_qkv[:, lanes(1)] = d_keys.astype(BF)
    d_values = d_values.astype(BF)
    d_qkv[:, lanes(2)] = d_values
    sums[0:1, lanes(1)] = jnp.sum(d_values.astype(F32), axis=0, keepdims=True)


def inputs_kernel(d_qkv, joined, part):
    part[...] = dot(d_qkv[...], joined[:, : d_qkv.shape[1]], NT).astype(BF)


def pack_kernel(w_qkv, w_out_t, unit_bias, norm_gain, norm_bias, attn):
    depth, cols, width = w_qkv.shape[1], w_qkv.shape[2], attn.shape[1]
    for kind in range(3):
        attn[:depth, kind * cols : (kind + 1) * cols] = w_qkv[kind]
    attn[:depth, 3 * cols :] = w_out_t[...]
    small = [ref[...].astype(F32) for ref in (unit_bias, norm_gain, norm_bias)]
    small = [jnp.pad(value, ((0, 0), (0, width - value.shape[1]))) for value in small]
    small.append(jnp.zeros((EXTRA - 7, width), F32))
    attn[depth:, :] = jnp.concatenate(small, axis=0).astype(BF)


def unpack_kernel(count, own, *refs):
    parts, (qkv, out, unit, gain, bias) = refs[:count], refs[count:]
    total = own[...]
    for part in parts:
        total = total + part[...].astype(F32)
    depth, cols = qkv.shape[1], qkv.shape[2]
    for kind in range(3):
        qkv[kind] = total[:depth, kind * cols : (kind + 1) * cols]
    out[...] = total[:depth, 3 * cols :].T
    extra = total[depth:]
    unit[...] = extra[0:1, : unit.shape[1]]
    gain[...] = extra[1:3, : gain.shape[1]]
    bias[...] = extra[3:7, : bias.shape[1]]


def unpack(own, parts, depth, cols, share, small):
    outs = [
        ((3, depth, cols), F32),
        ((cols, depth), F32),
        ((1, share), F32),
        ((2, small), F32),
        ((4, small), F32),
    ]
    if depth % 16 == 0:
        return call(functools.partial(unpack_kernel, len(parts)), outs, [own] + list(parts))
    total = total_of(own, parts)
    return (
        jnp.stack([total[:depth, t * cols : (t + 1) * cols] for t in range(3)]),
        total[:depth, 3 * cols :].T,
        total[depth : depth + 1, :share],
        total[depth + 1 : depth + 3, :small],
        total[depth + 3 : depth + 7, :small],
    )


def body(
    inputs, w_qkv, w_out, w_up, w_down, unit_bias, norm_gain, norm_bias, seq_lengths, cotangent
):
    place = Place()
    row, core = place.row, place.core
    groups = place.groups
    block, width = inputs.shape[1], inputs.shape[2]
    rows = 4 * block
    depth, head_cols = w_qkv.shape[1], w_qkv.shape[2]
    units = w_up.shape[1]
    share = unit_bias.shape[1]
    small = norm_gain.shape[1]
    cols = 2 * head_cols
    heads = cols // HD

    if depth % 16 == 0:
        (attn_shard,) = call(
            pack_kernel,
            [((depth + EXTRA, width), BF)],
            [w_qkv, w_out.T, unit_bias, norm_gain, norm_bias],
        )
    else:
        small_rows = [
            jnp.pad(part, ((0, 0), (0, width - part.shape[1]))) for part in (unit_bias, norm_gain, norm_bias)
        ]
        small_rows.append(jnp.zeros((EXTRA - 7, width), BF))
        attn_shard = jnp.concatenate([w_qkv[0], w_qkv[1], w_qkv[2], w_out.T], axis=1)
        attn_shard = jnp.concatenate([attn_shard] + small_rows, axis=0)
    keep = lambda array, index: lax.dynamic_index_in_dim(array, index, 0, keepdims=False)
    outgoing = jnp.stack([keep(inputs, 1 - row), keep(cotangent, 1 - row)])
    incoming = place.row_swap(outgoing)
    attn_own = jnp.stack(line_parts(place, after(attn_shard, outgoing)))
    attn_own = after(attn_own, incoming)
    attn_first, attn_second = place.cross(attn_own, 0), place.cross(attn_own, 1)
    up_own = jnp.stack(line_parts(place, after(w_up, attn_own)))
    attn_first = after(attn_first, attn_second, up_own)
    attn_far = place.cross(attn_first, 1)
    up_own = after(up_own, attn_first)
    up_first, up_second = place.cross(up_own, 0), place.cross(up_own, 1)
    down_own = jnp.stack(line_parts(place, after(w_down.T, up_own)))

    mine = jnp.stack([keep(inputs, row), keep(cotangent, row)])
    low_rows = jnp.where(row == 0, mine, incoming)
    high_rows = jnp.where(row == 0, incoming, mine)
    half = jnp.concatenate([low_rows, high_rows], axis=1)
    other = place.core_swap(half)
    both = jnp.where(
        core == 0,
        jnp.concatenate([half, other], axis=1),
        jnp.concatenate([other, half], axis=1),
    )
    x, grad_rows = both[0], both[1]

    attn_whole, extras, unit_bias = place_group(
        place, (attn_own, attn_first, attn_second, attn_far), depth, share
    )
    norm_here = extras[:, :, 1:7, :small]
    norm_there = place.core_swap(norm_here)
    norm_all = jnp.where(
        core == 0,
        jnp.stack([norm_here, norm_there], axis=2),
        jnp.stack([norm_there, norm_here], axis=2),
    )
    norm_all = jnp.transpose(norm_all, (3, 1, 0, 2, 4)).reshape(6, width).astype(F32)
    norms = jnp.pad(norm_all, ((0, 2), (0, 0)))
    table = place.roles()

    bounds = jnp.cumsum(keep(seq_lengths, row), dtype=jnp.int32)
    wide = rows * width
    joined, qkv = call(
        project_kernel,
        [((width, 4 * cols), BF), ((rows, 3 * cols), BF)],
        [x, attn_whole, unit_bias],
    )
    up_first = after(up_first, up_second, down_own, qkv)
    up_far = place.cross(up_first, 1)
    down_own = after(down_own, up_first)
    down_first, down_second = place.cross(down_own, 0), place.cross(down_own, 1)
    probs, ctx, part = call(
        functools.partial(attend_kernel, block, rows),
        [((heads, rows, rows), BF, True), ((rows, cols), BF), ((rows, width), BF)],
        [bounds, after(qkv, up_first, norms), joined],
        scalars=1,
        scratch=[pltpu.VMEM((rows, rows), F32)],
        steps=cols // LANES,
    )
    down_first = after(down_first, down_second, ctx)
    down_far = place.cross(down_first, 1)
    up_far = after(up_far, down_first)
    up_whole = place_group(place, (up_own, up_first, up_second, up_far), depth)[0]
    unit, rate, first_low, activated, slope = call(
        functools.partial(up_kernel, 2 * head_cols),
        [
            ((rows, width), BF, True),
            ((rows, LANES), F32, True),
            ((rows, width), BF, True),
            ((rows, 2 * units), BF, True),
            ((rows, 2 * units), BF, True),
        ],
        [(x, True), (part, True), (place.core_swap(part), True), norms, unit_bias, up_whole],
        steps=2,
    )
    part, down_whole = down(place, activated, (down_own, down_first, down_second, down_far), depth)
    result, d_mixed, totals_two = call(
        second_kernel,
        [((rows, width), BF, True), ((rows, width), BF, True), ((8, width), F32)],
        [(first_low, True), (part, True), (place.core_swap(part), True), (grad_rows, True), norms],
        steps=2,
    )

    down_own, down_first, down_second, down_far = outer(place, table, d_mixed, activated, depth)
    down_got_far = place.cross(down_far, 0)
    d_hidden, part, up_sums = call(
        hidden_back_kernel,
        [((rows, 2 * units), BF, True), ((rows, width), BF, True), ((8, 2 * units), F32)],
        [(after(d_mixed, down_far), True), down_whole, up_whole, (slope, True)],
        steps=2,
    )
    add = lambda one, other: (one.astype(F32) + other.astype(F32)).astype(BF)
    add_three = lambda one, two, three: one.astype(F32) + two.astype(F32) + three.astype(F32)
    up_own, up_first, up_second, up_far = outer(place, table, first_low, d_hidden, depth)
    down_second = add(down_second, after(down_got_far, up_far))
    down_got_second = place.cross(down_second, 1)
    down_got_first = place.cross(after(down_first, down_far), 0)
    up_got_far = place.cross(after(up_far, down_second), 0)
    d_att, d_ctx, totals_one = call(
        first_back_kernel,
        [((rows, width), BF, True), ((rows, cols), BF, True), ((8, width), F32)],
        [
            (after(d_mixed, down_second), True),
            (part, True),
            (place.core_swap(part), True),
            (unit, True),
            (rate, True),
            norms,
            joined,
        ],
        steps=2,
    )
    d_qkv, attn_sums = call(
        functools.partial(attend_back_kernel, rows),
        [((rows, 3 * cols), BF), ((8, 2 * cols), F32)],
        [d_ctx, qkv, (probs, True), ctx],
        scratch=[pltpu.VMEM((2, rows, rows), BF)],
        steps=cols // LANES,
    )
    attn_own, attn_first, attn_second, attn_far = outer_attn(
        place, table, x, d_qkv, d_att, ctx,
        (attn_sums, up_sums, totals_one, totals_two), depth,
    )
    attn_got_far = place.cross(attn_far, 0)
    up_second = add(up_second, after(up_got_far, attn_far))
    up_got_second = place.cross(up_second, 1)
    up_got_first = place.cross(after(up_first, up_second), 0)
    down_sum = add_three(down_own, down_got_first, after(down_got_second, up_second))
    down_parts = scatter_parts(place, down_sum)
    (part,) = call(
        inputs_kernel,
        [((rows, width), BF, True)],
        [(after(d_qkv, down_sum), True), joined],
        steps=2,
    )
    grad_in = d_att.astype(F32) + part.astype(F32) + place.core_swap(part).astype(F32)
    attn_second = add(attn_second, after(attn_got_far, part))
    attn_got_second = place.cross(attn_second, 1)
    attn_got_first = place.cross(after(attn_first, attn_second), 0)
    grad_down = total_of(down_sum[0], down_parts)
    up_sum = add_three(up_own, up_got_first, after(up_got_second, attn_second))
    up_parts = scatter_parts(place, up_sum)
    attn_sum = add_three(attn_own, after(attn_got_first, *down_parts, *up_parts), attn_got_second)
    attn_start, attn_parts = attn_sum[0], scatter_parts(place, attn_sum)
    grad_up = total_of(up_sum[0], up_parts)

    def hand_back(full):
        mine = lax.dynamic_slice_in_dim(full, core * 2 * block, 2 * block, 0)
        mine = mine.reshape(2, block, width)
        kept = keep(mine, row)
        got = place.row_swap(after(keep(mine, 1 - row).astype(BF), attn_sum)).astype(full.dtype)
        return jnp.where(row == 0, jnp.stack([kept, got]), jnp.stack([got, kept]))

    outputs, grad_inputs = hand_back(result), hand_back(grad_in)
    attn_parts = [after(part, outputs, grad_inputs) for part in attn_parts]
    grad_qkv, grad_out, grad_unit, grad_gain, grad_bias = unpack(
        attn_start, attn_parts, depth, head_cols, share, small
    )
    return (
        outputs,
        grad_inputs,
        grad_qkv,
        grad_out,
        grad_up,
        jnp.transpose(grad_down),
        grad_unit,
        grad_gain,
        grad_bias,
    )


def solution(mesh):
    placed = (
        P("dp", "mp", None),
        P(None, "dp", "mp"),
        P("mp", "dp"),
        P("dp", "mp"),
        P("mp", "dp"),
        P("mp", "dp"),
        P(None, ("dp", "mp")),
        P(None, ("dp", "mp")),
        P("dp", None),
        P("dp", "mp", None),
    )
    return jax.shard_map(
        body,
        mesh=mesh,
        in_specs=placed,
        out_specs=(
            P("dp", "mp", None),
            P("dp", "mp", None),
            P(None, "dp", "mp"),
            P("mp", "dp"),
            P("dp", "mp"),
            P("mp", "dp"),
            P("mp", "dp"),
            P(None, ("dp", "mp")),
            P(None, ("dp", "mp")),
        ),
        check_vma=False,
    )
```
